128 devices in a mesh: batch: 2 (over core), table: 64 (over y, x, z).
Axes of the slice: x: 4, y: 4, z: 4, core: 2. Of those that a mesh axis runs over, the one named last changes fastest.
Arguments:
- gate_pre: bfloat16 [32768, 4096], P(('batch', 'table')), may hold values from -6 to 6
- pick_logits: float32 [32768, 32], P(('batch', 'table')), may hold values from -8 to 260
- requests: int32 [2048, 64], P(('batch', 'table')), may hold values from -1 to 127, as said below
- slot_of_pick: int32 [32768, 32], P(('batch', 'table')), may hold values from 0 to 1023, as said below
- values: bfloat16 [8192, 4096], P('table'), may hold values from -6 to 6
- first_moment: float32 [8192, 4096], P('table'), may hold values from -2 to 2
- second_moment: float32 [8192, 4096], P('table'), may hold values from 0.01 to 1
- out_grad: bfloat16 [32768, 4096], P(('batch', 'table')), may hold values from -24 to 24
Outputs:
- layer_out: bfloat16 [32768, 4096], P(('batch', 'table'))
- gate_grad: bfloat16 [32768, 4096], P(('batch', 'table'))
- logit_grad: float32 [32768, 32], P(('batch', 'table'))
- value_next: bfloat16 [8192, 4096], P('table')
- first_next: float32 [8192, 4096], P('table')
- second_next: float32 [8192, 4096], P('table')
The draws below stay inside these ranges and needn't reach their ends.
Inputs may be any that keep to these rules, and one draw needn't show every extreme that they name: `requests`: row d * 16 + j, column p holds the j-th of the distinct rows, numbered within owner p's block of 128 rows, that device d of the batch+table order asks owner p for, or -1. Each device asks each owner for 2 to 16 rows, listed first in its column. In every draw some owner gets 16 rows from every device, and some device asks 16 rows of every owner. `slot_of_pick`: entry (i, k) names slot j * 64 + p of token i's own device, that is the entry of requests in row d * 16 + j, column p, which is never -1. The 32 slots of a token differ, and every entry of a device's requests that is not -1 is named by some pick of that device's tokens.
All inputs are finite; a program needn't handle non-finite values.
Results may differ from the reference program's by a relative error of at most 0.0071.
Values may be sent and summed in bfloat16 or wider, within the bound.
No kernel may reach another device: no remote copies, remote signals or barrier semaphores. Data moves between devices by JAX's collectives and lax.ppermute only.
A program may use at most 192 MiB of HBM per device.

```python
import math
import jax
import jax.numpy as jnp
from jax import lax

D = 4096
K = 32
CAP = 16
TOK_DEV = 256
ROW_DEV = 128
TOKENS = 32768
ROWS = 8192
SLOTS = 1024
N_TABLE = 64


def plan_picks(key):
    device_count = TOKENS // TOK_DEV
    table_count = SLOTS // CAP
    key_list = jax.random.split(key, 9)
    positions = jnp.arange(ROW_DEV, dtype=jnp.int32)
    owner_ids = jnp.arange(table_count, dtype=jnp.int32)
    device_ids = jnp.arange(device_count, dtype=jnp.int32)
    hot_owner = jax.random.randint(key_list[0], (), 0, table_count, dtype=jnp.int32)
    heavy_device = jax.random.randint(key_list[1], (), 0, device_count, dtype=jnp.int32)
    base_counts = jax.random.randint(key_list[2], (device_count, table_count), 2, CAP + 1, dtype=jnp.int32)
    divisor = 1 + (jax.random.randint(key_list[3], (table_count,), 0, 3, dtype=jnp.int32) == 0).astype(jnp.int32)
    counts = jnp.maximum(base_counts // divisor[None, :], 2)
    full_mask = (owner_ids[None, :] == hot_owner) | (device_ids[:, None] == heavy_device)
    counts = jnp.where(full_mask, CAP, counts).astype(jnp.int32)
    order_scores = jax.random.randint(key_list[4], (table_count, ROW_DEV), 0, 65536, dtype=jnp.int32) * ROW_DEV + positions[None, :]
    row_order = jnp.argsort(order_scores, axis=1).astype(jnp.int32)
    active = jax.random.randint(key_list[5], (table_count,), CAP, ROW_DEV + 1, dtype=jnp.int32)
    scores = jax.random.randint(key_list[6], (device_count, table_count, ROW_DEV), 0, 65536, dtype=jnp.int32) * ROW_DEV + positions
    scores = jnp.where(positions[None, None, :] < active[None, :, None], scores, 2 ** 30 + positions)
    chosen = jnp.argsort(scores, axis=2)[:, :, :CAP].astype(jnp.int32)
    chosen_rows = row_order[owner_ids[None, :, None], chosen]
    entries = jnp.arange(CAP, dtype=jnp.int32)
    lists_full = jnp.where(entries[None, None, :] < counts[:, :, None], chosen_rows, -1)
    requests = jnp.transpose(lists_full, (0, 2, 1)).reshape(device_count * CAP, table_count)
    listed_mask = (entries[None, :, None] < counts[:, None, :]).reshape(device_count, SLOTS)
    slot_ids = jnp.arange(SLOTS, dtype=jnp.int32)
    slot_scores = jax.random.randint(key_list[7], (device_count, SLOTS), 0, 65536, dtype=jnp.int32) * SLOTS + slot_ids
    slot_scores = jnp.where(listed_mask, slot_scores, 2 ** 30 + slot_ids)
    listed = jnp.argsort(slot_scores, axis=1).astype(jnp.int32)
    totals = jnp.sum(counts, axis=1)
    columns = jnp.arange(K, dtype=jnp.int32)
    lower_bound = columns[None, :] * totals[:, None] // K
    upper_bound = (columns[None, :] + 1) * totals[:, None] // K
    token_ids = jnp.arange(TOK_DEV, dtype=jnp.int32)
    token_scores = jax.random.randint(key_list[8], (device_count, K, TOK_DEV), 0, 65536, dtype=jnp.int32) * TOK_DEV + token_ids
    token_order = jnp.argsort(token_scores, axis=2).astype(jnp.int32)
    chosen_u = lower_bound[:, :, None] + token_order % (upper_bound - lower_bound)[:, :, None]
    slot_list = jnp.take_along_axis(listed, chosen_u.reshape(device_count, K * TOK_DEV), axis=1)
    slot_of_pick = jnp.transpose(slot_list.reshape(device_count, K, TOK_DEV), (0, 2, 1)).reshape(device_count * TOK_DEV, K)
    return (requests.astype(jnp.int32), slot_of_pick.astype(jnp.int32))


def draw_requests(key, part):
    requests, slot_list = plan_picks(key)
    return requests


def draw_slot_of_pick(key, part):
    requests, slot_list = plan_picks(key)
    return slot_list


def draw_pick_logits(key, part):
    key = jax.random.fold_in(key, 11)
    key_list = jax.random.split(key, 1)
    logits = jnp.clip(2.0 * jax.random.normal(key_list[0], (TOKENS, K), jnp.float32), -8.0, 8.0)
    return logits.astype(jnp.float32)


def shard_levels(own_key, dims, pieces, smallest, high):
    loudness = 1.0
    for dim, blocks in pieces:
        draws = jax.random.uniform(jax.random.fold_in(jax.random.fold_in(own_key, 6), dim), (blocks,), jnp.float32, smallest / len(pieces), high / len(pieces))
        loudness = loudness * jnp.repeat(jnp.exp(draws), dims[dim] // blocks).reshape((-1,) + (1,) * (len(dims) - 1 - dim))
    return loudness


def bell_draw(own_key, dims, deviation, reach, shards=(), held_as=jnp.bfloat16):
    result = jax.random.normal(own_key, dims, jnp.float32) * deviation
    if len(shards) > 0:
        result = shard_levels(own_key, dims, shards, -0.22, 0.18) * result
    return jnp.clip(result, min=-reach, max=reach).astype(held_as)


def setup_inputs(seed: int = 0) -> dict:
    seeds = jax.random.split(jax.random.key(seed), 9)
    return {
        "gate_pre": bell_draw(seeds[0], (TOKENS, D), 1.0, 6.0, ((0, 128),)),
        "pick_logits": draw_pick_logits(jax.random.fold_in(seeds[8], 71), 0),
        "requests": draw_requests(jax.random.fold_in(seeds[8], 71), 0),
        "slot_of_pick": draw_slot_of_pick(jax.random.fold_in(seeds[8], 71), 0),
        "values": bell_draw(seeds[4], (ROWS, D), 1.0, 6.0, ((0, 64),)),
        "first_moment": bell_draw(seeds[5], (ROWS, D), 0.3, 2.0, ((0, 64),), jnp.float32),
        "second_moment": jnp.clip(jnp.exp(math.log(1.0) - 4.6051702 * jax.random.uniform(seeds[6], (ROWS, D), jnp.float32) ** shard_levels(seeds[6], (ROWS, D), ((0, 64),), -0.2, 0.2)), 0.01, 1.0),
        "out_grad": bell_draw(seeds[7], (TOKENS, D), 4.0, 24.0, ((0, 128),)),
    }


learn_rate = 0.001

def reference(gate_pre, pick_logits, requests, slot_of_pick, values, first_moment, second_moment, out_grad):
    device_count = TOKENS // TOK_DEV
    weights = jax.nn.softmax(pick_logits, axis=-1)
    pick_weight = weights.astype(jnp.bfloat16)
    owner_ids = jnp.arange(N_TABLE, dtype=jnp.int32)
    request_lists = requests.reshape(device_count, CAP, N_TABLE)
    global_rows = jnp.where(request_lists >= 0, owner_ids[None, None, :] * ROW_DEV + request_lists, -1)
    global_rows = global_rows.reshape(device_count, SLOTS).astype(jnp.int32)

    def device_step(row_grad, inputs):
        gate_part, weight_part, slot_part, rows_part, grad_part, soft_part = inputs
        pick_row = jnp.take(rows_part, slot_part, axis=0).astype(jnp.int32)
        picked = jnp.where((pick_row >= 0)[..., None], values[jnp.maximum(pick_row, 0)], jnp.zeros((), jnp.bfloat16))
        picked_wide = picked.astype(jnp.float32)
        weight_wide = weight_part.astype(jnp.float32)
        memory = jnp.einsum('tk,tkd->td', weight_wide, picked_wide)
        gate_wide = gate_part.astype(jnp.float32)
        sigmoid_gate = jax.nn.sigmoid(gate_wide)
        silu_gate = gate_wide * sigmoid_gate
        grad_wide = grad_part.astype(jnp.float32)
        layer_out = (silu_gate * memory).astype(jnp.bfloat16)
        gated = (grad_wide * silu_gate).astype(jnp.bfloat16)
        gate_grad = (grad_wide * memory * sigmoid_gate * (1.0 + gate_wide * (1.0 - sigmoid_gate))).astype(jnp.bfloat16)
        gated_wide = gated.astype(jnp.float32)
        pick_score = jnp.einsum('td,tkd->tk', gated_wide, picked_wide)
        logit_grad = soft_part * (pick_score - lax.optimization_barrier(jnp.sum(soft_part * pick_score, axis=-1, keepdims=True)))
        pick_terms = weight_wide[..., None] * gated_wide[:, None, :]
        target = jnp.where(pick_row >= 0, pick_row, ROWS).reshape(-1)
        row_grad = row_grad.at[target].add(pick_terms.reshape(-1, D), mode='drop')
        return (row_grad, (layer_out, gate_grad, logit_grad))
    inputs = (gate_pre.reshape(device_count, TOK_DEV, D), pick_weight.reshape(device_count, TOK_DEV, K), slot_of_pick.reshape(device_count, TOK_DEV, K), global_rows, out_grad.reshape(device_count, TOK_DEV, D), weights.reshape(device_count, TOK_DEV, K))
    row_grad, results = lax.scan(device_step, jnp.zeros((ROWS, D), jnp.float32), inputs)
    layer_out, gate_grad, logit_grad = results
    all_rows = global_rows.reshape(-1)
    touch_count = jnp.zeros((ROWS,), jnp.float32).at[jnp.where(all_rows >= 0, all_rows, ROWS)].add(1.0, mode='drop')
    touched = (touch_count > 0.0)[:, None]
    first_new = 0.9 * first_moment + 0.1 * row_grad
    second_new = 0.95 * second_moment + 0.05 * row_grad * row_grad
    value_new = (values.astype(jnp.float32) - learn_rate * first_new / (jnp.sqrt(second_new) + 1e-08)).astype(jnp.bfloat16)
    value_next = jnp.where(touched, value_new, values)
    first_next = jnp.where(touched, first_new, first_moment)
    second_next = jnp.where(touched, second_new, second_moment)
    return (layer_out.reshape(TOKENS, D), gate_grad.reshape(TOKENS, D), logit_grad.reshape(TOKENS, K), value_next, first_next, second_next)
```

```python
import functools

import jax
import jax.numpy as jnp
from jax import lax
from jax.experimental import pallas as pl
from jax.experimental.pallas import tpu as pltpu
from jax.sharding import PartitionSpec as P

learn_rate = 0.001
LANES = 128
COLS = 512
RING = 4
CAPACITY = 16
CUBE = 8
BITS = (4, 2, 1)
ORDERS = ((0, 1, 2), (1, 2, 0), (2, 0, 1))
VMEM_BYTES = 60 * 1024 * 1024


WIDTH = 4096
CHUNK = 768
ROW_BLOCK = LANES


def chunk_width(chunk, total):
    return min(CHUNK, total - chunk * CHUNK)


def slot_place(owner, shift):
    spot = (owner // RING**2, owner // RING % RING, owner % RING)
    places = []
    for core in range(2):
        shifted = [(one + core) % RING for one in spot]
        cube = sum(bit * (one // 2) for bit, one in zip(BITS, shifted))
        chip = sum(bit * (one % 2) for bit, one in zip(BITS, shifted))
        places.append((cube, chip))
    (cube_0, chip_0), (cube_1, chip_1) = places
    cube = cube_0 + shift * (cube_1 - cube_0)
    chip = chip_0 + shift * (chip_1 - chip_0)
    return cube, chip


def pack_kernel(logit_ref, slot_ref, packed_ref, weight_ref):
    tokens, picks = logit_ref.shape
    slot_count = packed_ref.shape[1]
    logits = logit_ref[...]
    raised = jnp.exp(logits - jnp.max(logits, axis=-1, keepdims=True))
    weight_ref[...] = raised / jnp.sum(raised, axis=-1, keepdims=True)
    rows = 16

    @pl.loop(0, tokens // rows)
    def _(step):
        here = pl.ds(pl.multiple_of(step * rows, rows), rows)
        weight = weight_ref[here, :]
        slot = slot_ref[here, :]
        lane = lax.broadcasted_iota(jnp.int32, (rows, slot_count), 1)
        total = jnp.zeros((rows, slot_count), jnp.float32)
        for k in range(picks):
            total = jnp.where(lane == slot[:, k : k + 1], weight[:, k : k + 1], total)
        packed_ref[here, :] = total.astype(jnp.bfloat16)


def pack_call(logits, slot, slot_count):
    tokens, picks = logits.shape
    return pl.pallas_call(
        pack_kernel,
        out_shape=[
            jax.ShapeDtypeStruct((tokens, slot_count), jnp.bfloat16),
            jax.ShapeDtypeStruct((tokens, picks), jnp.float32),
        ],
        compiler_params=pltpu.CompilerParams(vmem_limit_bytes=VMEM_BYTES),
        cost_estimate=pl.CostEstimate(
            flops=2**25, bytes_accessed=2**20, transcendentals=tokens * picks
        ),
        name="pack_weights",
    )(logits, slot)


def gated_kernel(core_ref, gate_a, grad_a, gate_b, grad_b, mine_ref, theirs_ref):
    for gate_ref, grad_ref, out_ref in ((gate_a, grad_a, mine_ref), (gate_b, grad_b, theirs_ref)):
        gate = gate_ref[...].astype(jnp.float32)
        silu = gate * jax.nn.sigmoid(gate)
        out_ref[...] = (grad_ref[...].astype(jnp.float32) * silu).astype(jnp.bfloat16)


def gated_call(core, gate, grad):
    tokens, width = gate.shape
    steps = width // 2 // COLS
    mine = pl.BlockSpec((tokens, COLS), lambda i, core: (0, core[0] * steps + i))
    theirs = pl.BlockSpec((tokens, COLS), lambda i, core: (0, (1 - core[0]) * steps + i))
    half = pl.BlockSpec((tokens, COLS), lambda i, core: (0, i))
    return pl.pallas_call(
        gated_kernel,
        grid_spec=pltpu.PrefetchScalarGridSpec(
            num_scalar_prefetch=1,
            grid=(steps,),
            in_specs=[mine, mine, theirs, theirs],
            out_specs=[half, half],
        ),
        out_shape=[jax.ShapeDtypeStruct((tokens, width // 2), jnp.bfloat16)] * 2,
        compiler_params=pltpu.CompilerParams(vmem_limit_bytes=VMEM_BYTES),
        cost_estimate=pl.CostEstimate(
            flops=4 * tokens * width, bytes_accessed=6 * tokens * width, transcendentals=tokens * width
        ),
        name="gated_halves",
    )(core, gate, grad, gate, grad)


def slot_grad_kernel(
    core_ref, list_ref, packed_ref, packed_other_ref, gated_ref, gated_other_ref, slot_grad_ref
):
    owners = packed_ref.shape[1] // CAPACITY
    groups = ((packed_ref, gated_ref), (packed_other_ref, gated_other_ref))
    for group, (weights, gated) in enumerate(groups):
        found = lax.dot_general(
            weights[...], gated[...], (((0,), (0,)), ((), ())), preferred_element_type=jnp.float32
        ).astype(jnp.bfloat16)
        for owner in range(owners):
            cube, chip = slot_place(owner, core_ref[0])
            start = (cube * 2 + group) * ROW_BLOCK + chip * CAPACITY
            slot_grad_ref[pl.ds(pl.multiple_of(start, CAPACITY), CAPACITY), :] = found[
                owner * CAPACITY : (owner + 1) * CAPACITY, :
            ]

    @pl.when(pl.program_id(0) == pl.num_programs(0) - 1)
    def _():
        ones = jnp.ones((LANES, LANES), jnp.bfloat16)
        row = lax.broadcasted_iota(jnp.int32, (LANES, LANES), 0)
        lane = lax.broadcasted_iota(jnp.int32, (LANES, LANES), 1)
        start = WIDTH // 2 - (len(ORDERS) - 1) * CHUNK
        for block in range(list_ref.shape[0]):
            diagonal = jnp.where(row == lane, list_ref[block : block + 1, :], 0.0)
            slot_grad_ref[block * LANES : (block + 1) * LANES, start : start + LANES] = jnp.dot(
                diagonal.astype(jnp.bfloat16), ones, preferred_element_type=jnp.float32
            ).astype(jnp.bfloat16)


def slot_grad_call(core, lists, packed, packed_other, gated, gated_other):
    tokens, half = gated.shape
    slot_count = packed.shape[1]
    whole = lambda i: (0, 0)
    by_cols = lambda i: (0, i)
    weights = pl.BlockSpec((tokens, slot_count), whole)
    columns = pl.BlockSpec((tokens, CHUNK), by_cols)
    return pl.pallas_call(
        slot_grad_kernel,
        grid=(len(ORDERS),),
        in_specs=[
            pl.BlockSpec(memory_space=pltpu.SMEM),
            pl.BlockSpec(lists.shape, whole),
            weights, weights, columns, columns,
        ],
        out_specs=pl.BlockSpec((2 * slot_count, CHUNK), by_cols),
        out_shape=jax.ShapeDtypeStruct((2 * slot_count, half + LANES), jnp.bfloat16),
        compiler_params=pltpu.CompilerParams(vmem_limit_bytes=VMEM_BYTES),
        cost_estimate=pl.CostEstimate(
            flops=4 * tokens * slot_count * half, bytes_accessed=14 * 2**20, transcendentals=0
        ),
        name="slot_gradients",
    )(core, lists, packed, packed_other, gated, gated_other)


def relative(order, position):
    return sum(BITS[axis] for bit, axis in enumerate(order) if position >> bit & 1)


def asked_at(owner, peer, group):
    start = (peer * 2 + group) * ROW_BLOCK + owner * CAPACITY
    return pl.ds(pl.multiple_of(start, CAPACITY), CAPACITY)


def asked_rows(ref, owner, groups):
    return jnp.concatenate(
        [ref[asked_at(owner, peer, group), :] for peer in range(CUBE) for group in groups], axis=0
    )


def chosen_rows(id_ref, owner, groups):
    ids = asked_rows(id_ref, owner, groups)
    lane = lax.broadcasted_iota(jnp.int32, ids.shape, 1)
    return (ids.astype(jnp.float32) == lane.astype(jnp.float32)).astype(jnp.bfloat16)


def select_kernel(group, spot_ref, id_ref, *refs):
    out_ref = refs[-1]
    for chunk, order in enumerate(ORDERS):
        near, far = refs[2 * chunk], refs[2 * chunk + 1]
        rows = near.shape[0] * 2 // CUBE

        @pl.when(pl.program_id(0) == chunk)
        def _(order=order, near=near, far=far, rows=rows):
            for position in range(CUBE):
                source = near if position < CUBE // 2 else far
                start = position % (CUBE // 2) * rows
                owner = spot_ref[0] ^ relative(order, position)
                found = jnp.dot(
                    chosen_rows(id_ref, owner, (group,)),
                    source[start : start + rows, :],
                    preferred_element_type=jnp.float32,
                ).astype(jnp.bfloat16)
                for peer in range(CUBE):
                    at = pl.ds(
                        pl.multiple_of(peer * ROW_BLOCK + owner * CAPACITY, CAPACITY), CAPACITY
                    )
                    out_ref[at, : found.shape[1]] = found[peer * CAPACITY : (peer + 1) * CAPACITY, :]


def select_call(group, spot, arrived, parts):
    rows, wide = arrived.shape
    whole = lambda i: (0, 0)
    return pl.pallas_call(
        functools.partial(select_kernel, group),
        grid=(len(ORDERS),),
        in_specs=[
            pl.BlockSpec(memory_space=pltpu.SMEM),
            pl.BlockSpec((rows, LANES), lambda i: (0, wide // LANES - 1)),
        ]
        + [pl.BlockSpec(part.shape, whole) for part in parts],
        out_specs=pl.BlockSpec((rows // 2, CHUNK), lambda i: (0, i)),
        out_shape=jax.ShapeDtypeStruct((rows // 2, wide - LANES), jnp.bfloat16),
        compiler_params=pltpu.CompilerParams(vmem_limit_bytes=VMEM_BYTES),
        cost_estimate=pl.CostEstimate(
            flops=rows * LANES * wide, bytes_accessed=3 * rows * wide, transcendentals=0
        ),
        name="select_rows",
    )(spot, arrived, *parts)


def partial_kernel(chunk, spot_ref, id_ref, arrived_ref, keep_ref, send_ref):
    rows = keep_ref.shape[0] * 2 // CUBE
    cols = keep_ref.shape[1]
    for position in range(CUBE):
        owner = spot_ref[0] ^ relative(ORDERS[chunk], position)
        chosen = chosen_rows(id_ref, owner, (0, 1))
        by_rows = (((0,), (0,)), ((), ()))
        total = lax.dot_general(
            chosen, asked_rows(arrived_ref, owner, (0, 1))[:, :cols], by_rows,
            preferred_element_type=jnp.float32,
        )
        target = keep_ref if position < CUBE // 2 else send_ref
        start = position % (CUBE // 2) * rows
        target[start : start + rows, :] = total.astype(target.dtype)
        if chunk == len(ORDERS) - 1:
            hits = lax.dot_general(
                chosen, jnp.ones(chosen.shape, jnp.bfloat16), by_rows, preferred_element_type=jnp.float32
            )
            target[start : start + rows, cols - LANES :] = hits.astype(target.dtype)


def partial_call(chunk, spot, arrived, row_count):
    rows, wide = arrived.shape
    cols = chunk_width(chunk, wide)
    half = CUBE // 2 * row_count
    whole = lambda i: (0, 0)
    return pl.pallas_call(
        functools.partial(partial_kernel, chunk),
        grid=(1,),
        in_specs=[
            pl.BlockSpec(memory_space=pltpu.SMEM),
            pl.BlockSpec((rows, LANES), lambda i: (0, wide // LANES - 1)),
            pl.BlockSpec((rows, CHUNK), lambda i: (0, chunk)),
        ],
        out_specs=[pl.BlockSpec((half, cols), whole)] * 2,
        out_shape=[
            jax.ShapeDtypeStruct((half, cols), jnp.float32),
            jax.ShapeDtypeStruct((half, cols), jnp.bfloat16),
        ],
        compiler_params=pltpu.CompilerParams(vmem_limit_bytes=VMEM_BYTES),
        cost_estimate=pl.CostEstimate(
            flops=2 * rows * LANES * cols, bytes_accessed=8 * rows * cols, transcendentals=0
        ),
        name="partial_sums",
    )(spot, arrived, arrived)


def adam_kernel(
    core_ref, hits_ref, own_ref, other_ref, value_ref, first_ref, second_ref,
    value_out, first_out, second_out,
):
    touched = hits_ref[...][:, :1] > 0.0
    own = pl.program_id(0) < pl.num_programs(0) // 2
    row_grad = jnp.where(own, own_ref[...], other_ref[...])
    first = first_ref[...]
    second = second_ref[...]
    value = value_ref[...].astype(jnp.float32)
    first_new = 0.9 * first + 0.1 * row_grad
    second_new = 0.95 * second + 0.05 * row_grad * row_grad
    value_new = value - learn_rate * first_new / (jnp.sqrt(second_new) + 1e-08)
    value_out[...] = jnp.where(touched, value_new, value).astype(jnp.bfloat16)
    first_out[...] = jnp.where(touched, first_new, first)
    second_out[...] = jnp.where(touched, second_new, second)


def adam_call(core, own, other, values, first, second):
    rows, width = values.shape
    steps = width // 2 // COLS
    columns = pl.BlockSpec(
        (rows, COLS),
        lambda i, core: (0, lax.rem(core[0] + i // steps, 2) * steps + lax.rem(i, steps)),
    )
    return pl.pallas_call(
        adam_kernel,
        grid_spec=pltpu.PrefetchScalarGridSpec(
            num_scalar_prefetch=1,
            grid=(2 * steps,),
            in_specs=[
                pl.BlockSpec((rows, LANES), lambda i, core: (0, width // 2 // LANES)),
                pl.BlockSpec((rows, COLS), lambda i, core: (0, jnp.minimum(i, steps - 1))),
                pl.BlockSpec((rows, COLS), lambda i, core: (0, jnp.maximum(i - steps, 0))),
                columns, columns, columns,
            ],
            out_specs=[columns] * 3,
        ),
        out_shape=[
            jax.ShapeDtypeStruct(values.shape, values.dtype),
            jax.ShapeDtypeStruct(first.shape, first.dtype),
            jax.ShapeDtypeStruct(second.shape, second.dtype),
        ],
        compiler_params=pltpu.CompilerParams(vmem_limit_bytes=VMEM_BYTES),
        cost_estimate=pl.CostEstimate(
            flops=10 * rows * width, bytes_accessed=28 * rows * width, transcendentals=rows * width
        ),
        name="adam_rows",
    )(core, own, own, other, values, first, second)


def read_kernel(own, core_ref, packed_ref, fetched_ref, gate_ref, grad_ref, *refs):
    if own:
        weight_ref, slot_ref, before_ref, _, _, out_ref, gate_grad_ref, logit_grad_ref = refs[:8]
    else:
        out_ref, gate_grad_ref, score_out_ref = refs[:3]
    ordered_ref, score_ref = refs[-2:]
    step = pl.program_id(0)
    shift = core_ref[0] if own else 1 - core_ref[0]
    for owner in range(ordered_ref.shape[0] // CAPACITY):
        cube, chip = slot_place(owner, shift)
        at = pl.ds(pl.multiple_of(cube * ROW_BLOCK + chip * CAPACITY, CAPACITY), CAPACITY)
        ordered_ref[owner * CAPACITY : (owner + 1) * CAPACITY, :] = fetched_ref[at, :]
    fetched = ordered_ref[...]
    memory = jnp.dot(packed_ref[...], fetched, preferred_element_type=jnp.float32)
    gate = gate_ref[...].astype(jnp.float32)
    sig = jax.nn.sigmoid(gate)
    silu = gate * sig
    grad = grad_ref[...].astype(jnp.float32)
    out_ref[...] = (silu * memory).astype(jnp.bfloat16)
    gated = (grad * silu).astype(jnp.bfloat16)
    gate_grad_ref[...] = (grad * memory * sig * (1.0 + gate * (1.0 - sig))).astype(jnp.bfloat16)
    score = lax.dot_general(
        gated, fetched, (((1,), (1,)), ((), ())), preferred_element_type=jnp.float32
    )

    @pl.when(step == 0)
    def _():
        score_ref[...] = score + before_ref[...] if own else score

    @pl.when(step > 0)
    def _():
        score_ref[...] += score

    @pl.when(step == pl.num_programs(0) - 1)
    def _():
        if not own:
            score_out_ref[...] = score_ref[...]
            return
        picks = weight_ref.shape[1]
        slot = slot_ref[...]
        low = lax.rem(slot, LANES)
        high = slot // LANES
        wide = jnp.zeros(slot.shape, jnp.float32)
        for part in range(score_ref.shape[1] // LANES):
            here = score_ref[:, part * LANES : (part + 1) * LANES]
            wide = jnp.where(high == part, jnp.take_along_axis(here, low, axis=1), wide)
        pick_score = wide[:, :picks]
        weight = weight_ref[...]
        mean_score = jnp.sum(weight * pick_score, axis=-1, keepdims=True)
        wide = jnp.pad(weight * (pick_score - mean_score), ((0, 0), (0, LANES - picks)))
        logit_grad_ref[...] = wide.T[:picks, :]


def read_call(core, packed, fetched, gate, grad, last=None):
    tokens, width = gate.shape
    slot_count = packed.shape[1]
    steps = width // 2 // COLS
    own = last is not None
    whole = lambda i, core: (0, 0)

    def by_cols(i, core):
        half = core[0] if own else 1 - core[0]
        return (0, half * steps + i)

    columns = pl.BlockSpec((tokens, COLS), by_cols)
    in_specs = [
        pl.BlockSpec((tokens, slot_count), whole),
        pl.BlockSpec((slot_count, COLS), lambda i, core: (0, i)),
        columns,
        columns,
    ]
    out_specs = [columns, columns]
    out_shape = [jax.ShapeDtypeStruct((tokens, width), jnp.bfloat16)] * 2
    args = [packed, fetched, gate, grad]
    aliases = {}
    if own:
        weight, slot, layer_out, gate_grad, score = last
        picks = weight.shape[1]
        slot = jnp.pad(slot, ((0, 0), (0, LANES - picks)))
        args += [weight, slot, score, layer_out, gate_grad]
        in_specs += [pl.BlockSpec(one.shape, whole) for one in (weight, slot, score)]
        in_specs += [pl.BlockSpec(memory_space=pl.ANY)] * 2
        out_specs.append(pl.BlockSpec((picks, tokens), whole))
        out_shape.append(jax.ShapeDtypeStruct((picks, tokens), jnp.float32))
        aliases = {8: 0, 9: 1}
    else:
        out_specs.append(pl.BlockSpec((tokens, slot_count), whole))
        out_shape.append(jax.ShapeDtypeStruct((tokens, slot_count), jnp.float32))
    return pl.pallas_call(
        functools.partial(read_kernel, own),
        grid_spec=pltpu.PrefetchScalarGridSpec(
            num_scalar_prefetch=1,
            grid=(steps,),
            in_specs=in_specs,
            out_specs=out_specs,
            scratch_shapes=[
                pltpu.VMEM((slot_count, COLS), jnp.bfloat16),
                pltpu.VMEM((tokens, slot_count), jnp.float32),
            ],
        ),
        out_shape=out_shape,
        input_output_aliases=aliases,
        compiler_params=pltpu.CompilerParams(vmem_limit_bytes=VMEM_BYTES),
        cost_estimate=pl.CostEstimate(
            flops=2 * tokens * slot_count * width, bytes_accessed=9 * 2**20, transcendentals=tokens * width // 2
        ),
        name="read_and_scores",
    )(core, *args)


def place_of(core, shifted):
    spot = [(one - core) % RING for one in shifted]
    return (spot[0] * RING + spot[1]) * RING + spot[2]


def shifted_of(core, index):
    return [(one + core) % RING for one in (index // RING**2, index // RING % RING, index % RING)]


def swap(x, axis):
    pairs = []
    for core in range(2):
        for index in range(RING**3):
            shifted = shifted_of(core, index)
            shifted[axis] ^= 1
            pairs.append((core * RING**3 + index, core * RING**3 + place_of(core, shifted)))
    return lax.ppermute(x, ("batch", "table"), pairs)


def swap_cores(x):
    return lax.ppermute(x, "batch", [(0, 1), (1, 0)])


def cube_exchange(x):
    groups = []
    for core in range(2):
        found = {}
        for index in range(RING**3):
            shifted = shifted_of(core, index)
            group = tuple((one + 1) % RING // 2 for one in shifted)
            order = sum(bit * (one // 2) for bit, one in zip(BITS, shifted))
            found.setdefault(group, {})[order] = core * RING**3 + index
        groups += [[members[n] for n in range(CUBE)] for _, members in sorted(found.items())]
    return lax.all_to_all(
        x, ("batch", "table"), split_axis=0, concat_axis=0, axis_index_groups=groups, tiled=True
    )


def after(first, then):
    count = len(first)
    return lax.optimization_barrier((*first, *then))[count:]


def local(
    gate_pre, pick_logits, requests, slot_of_pick, values, first_moment, second_moment, out_grad
):
    capacity, table_size = requests.shape
    slot_count = capacity * table_size
    row_count, width = values.shape
    half_width = width // 2
    core = lax.axis_index("batch")
    shifted = shifted_of(core, lax.axis_index("table"))
    inside = sum(bit * (one % 2) for bit, one in zip(BITS, shifted))
    spot = inside.astype(jnp.int32).reshape(1)
    which = core.astype(jnp.int32).reshape(1)

    mine = lax.dynamic_slice(values, (0, core * half_width), (row_count, half_width))
    parts = [mine[:, chunk * CHUNK : (chunk + 1) * CHUNK] for chunk in range(len(ORDERS))]
    swapped = [swap(part, order[0]) for part, order in zip(parts, ORDERS)]

    lists = jnp.stack([requests, swap_cores(requests)]).reshape(2, capacity, RING, RING, RING)
    for axis in range(2, 5):
        turned = jnp.concatenate(
            [lax.slice_in_dim(lists, RING - 1, RING, axis=axis), lax.slice_in_dim(lists, 0, RING - 1, axis=axis)],
            axis=axis,
        )
        lists = jnp.where(core == 0, lists, turned)
    lists = lists.reshape(2, capacity, 2, 2, 2, 2, 2, 2).transpose(2, 4, 6, 0, 3, 5, 7, 1)
    lists = lists.reshape(2 * CUBE, ROW_BLOCK).astype(jnp.float32)

    gated, gated_theirs = gated_call(which, gate_pre, out_grad)
    gated_other = swap_cores(gated_theirs)
    swapped = after([gated], swapped)
    parts = [jnp.concatenate(pair, axis=0) for pair in zip(parts, swapped)]
    swapped = [swap(part, order[1]) for part, order in zip(parts, ORDERS)]
    slot = (slot_of_pick % table_size) * capacity + slot_of_pick // table_size
    (slot,) = after(parts, [slot])
    packed, weight = pack_call(pick_logits, slot, slot_count)
    packed_other = swap_cores(packed)
    slot_grad = slot_grad_call(which, lists, packed, packed_other, gated, gated_other)
    swapped = after([slot_grad], swapped)
    (slot_grad,) = after(swapped, [slot_grad])
    arrived = cube_exchange(slot_grad)
    parts = [jnp.concatenate(pair, axis=0) for pair in zip(parts, swapped)]
    swapped = [swap(part, order[2]) for part, order in zip(parts, ORDERS)]
    gathered = [half for pair in zip(parts, swapped) for half in pair]
    (arrived,) = after(swapped, [arrived])

    found_other = select_call(1, spot, arrived, gathered)
    fetched_theirs = cube_exchange(found_other)
    (arrived,) = after([found_other], [arrived])
    found = select_call(0, spot, arrived, gathered)
    (arrived,) = after([found], [arrived])
    halves = [partial_call(chunk, spot, arrived, row_count) for chunk in range(len(ORDERS))]
    (fetched_theirs,) = after([keep for keep, _ in halves], [fetched_theirs])
    (found,) = after([fetched_theirs], [found])
    fetched = cube_exchange(found)
    fetched_other = swap_cores(fetched_theirs)

    received = [swap(send, order[2]) for (_, send), order in zip(halves, ORDERS)]
    half = CUBE // 4 * row_count
    for step in (1, 0):
        totals = [keep + other.astype(jnp.float32) for (keep, _), other in zip(halves, received)]
        halves = [(total[:half], total[half:].astype(jnp.bfloat16)) for total in totals]
        received = [swap(send, order[step]) for (_, send), order in zip(halves, ORDERS)]
        half //= 2
    (fetched_other,) = after([send for _, send in halves], [fetched_other])
    layer_out, gate_grad, score = read_call(which, packed, fetched_other, gate_pre, out_grad)
    received = after([score], received)
    totals = [keep + other.astype(jnp.float32) for (keep, _), other in zip(halves, received)]
    own = jnp.concatenate(totals, axis=1)
    value_next, first_next, second_next = adam_call(
        which, own, swap_cores(own), values, first_moment, second_moment
    )
    (fetched,) = after([value_next], [fetched])
    layer_out, gate_grad, logit_grad = read_call(
        which, packed, fetched, gate_pre, out_grad, (weight, slot, layer_out, gate_grad, score)
    )
    return (layer_out, gate_grad, logit_grad.T, value_next, first_next, second_next)


def solution(mesh):
    tokens = P(("batch", "table"), None)
    rows = P("table", None)
    return jax.shard_map(
        local,
        mesh=mesh,
        in_specs=(tokens, tokens, tokens, tokens, rows, rows, rows, tokens),
        out_specs=(tokens, tokens, tokens, rows, rows, rows),
        check_vma=False,
    )
```

```python
import functools

import jax
import jax.numpy as jnp
from jax import lax
from jax.experimental import pallas as pl
from jax.experimental.pallas import tpu as pltpu
from jax.sharding import PartitionSpec as P

learn_rate = 0.001
LANES = 128
COLS = 512
RING = 4
CAPACITY = 16
CUBE = 8
BITS = (4, 2, 1)
ORDERS = ((0, 1, 2), (1, 2, 0), (2, 0, 1))
VMEM_BYTES = 60 * 1024 * 1024


CHUNK = 768
ROW_BLOCK = LANES


def chunk_width(chunk, total):
    return min(CHUNK, total - chunk * CHUNK)


def slot_place(owner, shift):
    spot = (owner // RING**2, owner // RING % RING, owner % RING)
    places = []
    for core in range(2):
        shifted = [(one + core) % RING for one in spot]
        cube = sum(bit * (one // 2) for bit, one in zip(BITS, shifted))
        chip = sum(bit * (one % 2) for bit, one in zip(BITS, shifted))
        places.append((cube, chip))
    (cube_0, chip_0), (cube_1, chip_1) = places
    cube = cube_0 + shift * (cube_1 - cube_0)
    chip = chip_0 + shift * (chip_1 - chip_0)
    return cube, chip


def pack_kernel(logit_ref, slot_ref, packed_ref, weight_ref):
    tokens, picks = logit_ref.shape
    slot_count = packed_ref.shape[1]
    logits = logit_ref[...]
    raised = jnp.exp(logits - jnp.max(logits, axis=-1, keepdims=True))
    weight_ref[...] = raised / jnp.sum(raised, axis=-1, keepdims=True)
    rows = 16

    @pl.loop(0, tokens // rows)
    def _(step):
        here = pl.ds(pl.multiple_of(step * rows, rows), rows)
        weight = weight_ref[here, :]
        slot = slot_ref[here, :]
        lane = lax.broadcasted_iota(jnp.int32, (rows, slot_count), 1)
        total = jnp.zeros((rows, slot_count), jnp.float32)
        for k in range(picks):
            total = jnp.where(lane == slot[:, k : k + 1], weight[:, k : k + 1], total)
        packed_ref[here, :] = total.astype(jnp.bfloat16)


def pack_call(logits, slot, slot_count):
    tokens, picks = logits.shape
    return pl.pallas_call(
        pack_kernel,
        out_shape=[
            jax.ShapeDtypeStruct((tokens, slot_count), jnp.bfloat16),
            jax.ShapeDtypeStruct((tokens, picks), jnp.float32),
        ],
        compiler_params=pltpu.CompilerParams(vmem_limit_bytes=VMEM_BYTES),
        cost_estimate=pl.CostEstimate(
            flops=2**25, bytes_accessed=2**20, transcendentals=tokens * picks
        ),
        name="pack_weights",
    )(logits, slot)


def gated_kernel(core_ref, gate_a, grad_a, gate_b, grad_b, mine_ref, theirs_ref):
    for gate_ref, grad_ref, out_ref in ((gate_a, grad_a, mine_ref), (gate_b, grad_b, theirs_ref)):
        gate = gate_ref[...].astype(jnp.float32)
        silu = gate * jax.nn.sigmoid(gate)
        out_ref[...] = (grad_ref[...].astype(jnp.float32) * silu).astype(jnp.bfloat16)


def gated_call(core, gate, grad):
    tokens, width = gate.shape
    steps = width // 2 // COLS
    mine = pl.BlockSpec((tokens, COLS), lambda i, core: (0, core[0] * steps + i))
    theirs = pl.BlockSpec((tokens, COLS), lambda i, core: (0, (1 - core[0]) * steps + i))
    half = pl.BlockSpec((tokens, COLS), lambda i, core: (0, i))
    return pl.pallas_call(
        gated_kernel,
        grid_spec=pltpu.PrefetchScalarGridSpec(
            num_scalar_prefetch=1,
            grid=(steps,),
            in_specs=[mine, mine, theirs, theirs],
            out_specs=[half, half],
        ),
        out_shape=[jax.ShapeDtypeStruct((tokens, width // 2), jnp.bfloat16)] * 2,
        compiler_params=pltpu.CompilerParams(vmem_limit_bytes=VMEM_BYTES),
        cost_estimate=pl.CostEstimate(
            flops=4 * tokens * width, bytes_accessed=6 * tokens * width, transcendentals=tokens * width
        ),
        name="gated_halves",
    )(core, gate, grad, gate, grad)


def slot_grad_kernel(
    core_ref, packed_ref, packed_other_ref, gated_ref, gated_other_ref, slot_grad_ref, turned_ref
):
    slot_count = packed_ref.shape[1]
    groups = ((packed_ref, gated_ref), (packed_other_ref, gated_other_ref))

    @pl.when(pl.program_id(0) == 0)
    def _():
        for group, (weights, _) in enumerate(groups):
            turned_ref[group] = weights[...].T

    for group, (_, gated) in enumerate(groups):
        found = jnp.dot(
            turned_ref[group], gated[...], preferred_element_type=jnp.float32
        ).astype(jnp.bfloat16)
        for owner in range(slot_count // CAPACITY):
            cube, chip = slot_place(owner, core_ref[0])
            start = (cube * 2 + group) * ROW_BLOCK + chip * CAPACITY
            slot_grad_ref[pl.ds(pl.multiple_of(start, CAPACITY), CAPACITY), :] = found[
                owner * CAPACITY : (owner + 1) * CAPACITY, :
            ]


def slot_grad_call(core, packed, packed_other, gated, gated_other):
    tokens, half = gated.shape
    slot_count = packed.shape[1]
    whole = lambda i: (0, 0)
    by_cols = lambda i: (0, i)
    weights = pl.BlockSpec((tokens, slot_count), whole)
    columns = pl.BlockSpec((tokens, COLS), by_cols)
    return pl.pallas_call(
        slot_grad_kernel,
        grid=(half // COLS,),
        in_specs=[pl.BlockSpec(memory_space=pltpu.SMEM), weights, weights, columns, columns],
        out_specs=pl.BlockSpec((2 * slot_count, COLS), by_cols),
        out_shape=jax.ShapeDtypeStruct((2 * slot_count, half), jnp.bfloat16),
        scratch_shapes=[pltpu.VMEM((2, slot_count, tokens), jnp.bfloat16)],
        compiler_params=pltpu.CompilerParams(vmem_limit_bytes=VMEM_BYTES),
        cost_estimate=pl.CostEstimate(
            flops=4 * tokens * slot_count * half, bytes_accessed=14 * 2**20, transcendentals=0
        ),
        name="slot_gradients",
    )(core, packed, packed_other, gated, gated_other)


def spread_kernel(list_ref, spread_ref):
    ones = jnp.ones((LANES, LANES), jnp.bfloat16)
    row = lax.broadcasted_iota(jnp.int32, (LANES, LANES), 0)
    lane = lax.broadcasted_iota(jnp.int32, (LANES, LANES), 1)
    for block in range(list_ref.shape[0]):
        diagonal = jnp.where(row == lane, list_ref[block : block + 1, :], 0.0)
        spread_ref[block * LANES : (block + 1) * LANES, :] = jnp.dot(
            diagonal.astype(jnp.bfloat16), ones, preferred_element_type=jnp.float32
        ).astype(jnp.bfloat16)


def spread_call(lists):
    return pl.pallas_call(
        spread_kernel,
        out_shape=jax.ShapeDtypeStruct((lists.size, LANES), jnp.bfloat16),
        name="spread_lists",
    )(lists)


def relative(order, position):
    return sum(BITS[axis] for bit, axis in enumerate(order) if position >> bit & 1)


def asked_at(owner, peer, group):
    start = (peer * 2 + group) * ROW_BLOCK + owner * CAPACITY
    return pl.ds(pl.multiple_of(start, CAPACITY), CAPACITY)


def asked_rows(ref, owner, groups):
    return jnp.concatenate(
        [ref[asked_at(owner, peer, group), :] for peer in range(CUBE) for group in groups], axis=0
    )


def chosen_rows(id_ref, owner, groups):
    ids = asked_rows(id_ref, owner, groups)
    lane = lax.broadcasted_iota(jnp.int32, ids.shape, 1)
    return (ids.astype(jnp.float32) == lane.astype(jnp.float32)).astype(jnp.bfloat16)


def select_kernel(group, spot_ref, id_ref, *refs):
    out_ref = refs[-1]
    for chunk, order in enumerate(ORDERS):
        near, far = refs[2 * chunk], refs[2 * chunk + 1]
        rows = near.shape[0] * 2 // CUBE

        @pl.when(pl.program_id(0) == chunk)
        def _(order=order, near=near, far=far, rows=rows):
            for position in range(CUBE):
                source = near if position < CUBE // 2 else far
                start = position % (CUBE // 2) * rows
                owner = spot_ref[0] ^ relative(order, position)
                found = jnp.dot(
                    chosen_rows(id_ref, owner, (group,)),
                    source[start : start + rows, :],
                    preferred_element_type=jnp.float32,
                ).astype(jnp.bfloat16)
                for peer in range(CUBE):
                    at = pl.ds(
                        pl.multiple_of(peer * ROW_BLOCK + owner * CAPACITY, CAPACITY), CAPACITY
                    )
                    out_ref[at, : found.shape[1]] = found[peer * CAPACITY : (peer + 1) * CAPACITY, :]


def select_call(group, spot, ids, parts, half_width):
    rows, wide = ids.shape[0], half_width + LANES
    whole = lambda i: (0, 0)
    return pl.pallas_call(
        functools.partial(select_kernel, group),
        grid=(len(ORDERS),),
        in_specs=[
            pl.BlockSpec(memory_space=pltpu.SMEM),
            pl.BlockSpec(ids.shape, whole),
        ]
        + [pl.BlockSpec(part.shape, whole) for part in parts],
        out_specs=pl.BlockSpec((rows // 2, CHUNK), lambda i: (0, i)),
        out_shape=jax.ShapeDtypeStruct((rows // 2, wide - LANES), jnp.bfloat16),
        compiler_params=pltpu.CompilerParams(vmem_limit_bytes=VMEM_BYTES),
        cost_estimate=pl.CostEstimate(
            flops=rows * LANES * wide, bytes_accessed=3 * rows * wide, transcendentals=0
        ),
        name="select_rows",
    )(spot, ids, *parts)


def partial_kernel(chunk, spot_ref, id_ref, arrived_ref, keep_ref, send_ref):
    rows = keep_ref.shape[0] * 2 // CUBE
    cols = keep_ref.shape[1]
    for position in range(CUBE):
        owner = spot_ref[0] ^ relative(ORDERS[chunk], position)
        chosen = chosen_rows(id_ref, owner, (0, 1))
        by_rows = (((0,), (0,)), ((), ()))
        total = lax.dot_general(
            chosen, asked_rows(arrived_ref, owner, (0, 1))[:, :cols], by_rows,
            preferred_element_type=jnp.float32,
        )
        target = keep_ref if position < CUBE // 2 else send_ref
        start = position % (CUBE // 2) * rows
        target[start : start + rows, :] = total.astype(target.dtype)
        if chunk == len(ORDERS) - 1:
            hits = lax.dot_general(
                chosen, jnp.ones(chosen.shape, jnp.bfloat16), by_rows, preferred_element_type=jnp.float32
            )
            target[start : start + rows, cols - LANES :] = hits.astype(target.dtype)


def partial_call(chunk, spot, ids, arrived, row_count):
    rows, wide = arrived.shape[0], arrived.shape[1] + LANES
    cols = chunk_width(chunk, wide)
    half = CUBE // 2 * row_count
    whole = lambda i: (0, 0)
    return pl.pallas_call(
        functools.partial(partial_kernel, chunk),
        grid=(1,),
        in_specs=[
            pl.BlockSpec(memory_space=pltpu.SMEM),
            pl.BlockSpec(ids.shape, whole),
            pl.BlockSpec((rows, CHUNK), lambda i: (0, chunk)),
        ],
        out_specs=[pl.BlockSpec((half, cols), whole)] * 2,
        out_shape=[
            jax.ShapeDtypeStruct((half, cols), jnp.float32),
            jax.ShapeDtypeStruct((half, cols), jnp.bfloat16),
        ],
        compiler_params=pltpu.CompilerParams(vmem_limit_bytes=VMEM_BYTES),
        cost_estimate=pl.CostEstimate(
            flops=2 * rows * LANES * cols, bytes_accessed=8 * rows * cols, transcendentals=0
        ),
        name="partial_sums",
    )(spot, ids, arrived)


def adam_kernel(
    core_ref, hits_ref, own_ref, other_ref, value_ref, first_ref, second_ref,
    value_out, first_out, second_out,
):
    touched = hits_ref[...][:, :1] > 0.0
    own = pl.program_id(0) < pl.num_programs(0) // 2
    row_grad = jnp.where(own, own_ref[...], other_ref[...])
    first = first_ref[...]
    second = second_ref[...]
    value = value_ref[...].astype(jnp.float32)
    first_new = 0.9 * first + 0.1 * row_grad
    second_new = 0.95 * second + 0.05 * row_grad * row_grad
    value_new = value - learn_rate * first_new / (jnp.sqrt(second_new) + 1e-08)
    value_out[...] = jnp.where(touched, value_new, value).astype(jnp.bfloat16)
    first_out[...] = jnp.where(touched, first_new, first)
    second_out[...] = jnp.where(touched, second_new, second)


def adam_call(core, own, other, values, first, second):
    rows, width = values.shape
    steps = width // 2 // COLS
    columns = pl.BlockSpec(
        (rows, COLS),
        lambda i, core: (0, lax.rem(core[0] + i // steps, 2) * steps + lax.rem(i, steps)),
    )
    return pl.pallas_call(
        adam_kernel,
        grid_spec=pltpu.PrefetchScalarGridSpec(
            num_scalar_prefetch=1,
            grid=(2 * steps,),
            in_specs=[
                pl.BlockSpec((rows, LANES), lambda i, core: (0, width // 2 // LANES)),
                pl.BlockSpec((rows, COLS), lambda i, core: (0, jnp.minimum(i, steps - 1))),
                pl.BlockSpec((rows, COLS), lambda i, core: (0, jnp.maximum(i - steps, 0))),
                columns, columns, columns,
            ],
            out_specs=[columns] * 3,
        ),
        out_shape=[
            jax.ShapeDtypeStruct(values.shape, values.dtype),
            jax.ShapeDtypeStruct(first.shape, first.dtype),
            jax.ShapeDtypeStruct(second.shape, second.dtype),
        ],
        compiler_params=pltpu.CompilerParams(vmem_limit_bytes=VMEM_BYTES),
        cost_estimate=pl.CostEstimate(
            flops=10 * rows * width, bytes_accessed=28 * rows * width, transcendentals=rows * width
        ),
        name="adam_rows",
    )(core, own, own, other, values, first, second)


def read_kernel(own, core_ref, packed_ref, fetched_ref, gate_ref, grad_ref, *refs):
    if own:
        weight_ref, slot_ref, before_ref, _, _, out_ref, gate_grad_ref, logit_grad_ref = refs[:8]
    else:
        out_ref, gate_grad_ref, score_out_ref = refs[:3]
    ordered_ref, score_ref = refs[-2:]
    step = pl.program_id(0)
    shift = core_ref[0] if own else 1 - core_ref[0]
    for owner in range(ordered_ref.shape[0] // CAPACITY):
        cube, chip = slot_place(owner, shift)
        at = pl.ds(pl.multiple_of(cube * ROW_BLOCK + chip * CAPACITY, CAPACITY), CAPACITY)
        ordered_ref[owner * CAPACITY : (owner + 1) * CAPACITY, :] = fetched_ref[at, :]
    fetched = ordered_ref[...]
    memory = jnp.dot(packed_ref[...], fetched, preferred_element_type=jnp.float32)
    gate = gate_ref[...].astype(jnp.float32)
    sig = jax.nn.sigmoid(gate)
    silu = gate * sig
    grad = grad_ref[...].astype(jnp.float32)
    out_ref[...] = (silu * memory).astype(jnp.bfloat16)
    gated = (grad * silu).astype(jnp.bfloat16)
    gate_grad_ref[...] = (grad * memory * sig * (1.0 + gate * (1.0 - sig))).astype(jnp.bfloat16)
    score = lax.dot_general(
        gated, fetched, (((1,), (1,)), ((), ())), preferred_element_type=jnp.float32
    )

    @pl.when(step == 0)
    def _():
        score_ref[...] = score + before_ref[...] if own else score

    @pl.when(step > 0)
    def _():
        score_ref[...] += score

    @pl.when(step == pl.num_programs(0) - 1)
    def _():
        if not own:
            score_out_ref[...] = score_ref[...]
            return
        picks = weight_ref.shape[1]
        slot = slot_ref[...]
        low = lax.rem(slot, LANES)
        high = slot // LANES
        wide = jnp.zeros(slot.shape, jnp.float32)
        for part in range(score_ref.shape[1] // LANES):
            here = score_ref[:, part * LANES : (part + 1) * LANES]
            wide = jnp.where(high == part, jnp.take_along_axis(here, low, axis=1), wide)
        pick_score = wide[:, :picks]
        weight = weight_ref[...]
        mean_score = jnp.sum(weight * pick_score, axis=-1, keepdims=True)
        wide = jnp.pad(weight * (pick_score - mean_score), ((0, 0), (0, LANES - picks)))
        logit_grad_ref[...] = wide.T[:picks, :]


def read_call(core, packed, fetched, gate, grad, last=None):
    tokens, width = gate.shape
    slot_count = packed.shape[1]
    steps = width // 2 // COLS
    own = last is not None
    whole = lambda i, core: (0, 0)

    def by_cols(i, core):
        half = core[0] if own else 1 - core[0]
        return (0, half * steps + i)

    columns = pl.BlockSpec((tokens, COLS), by_cols)
    in_specs = [
        pl.BlockSpec((tokens, slot_count), whole),
        pl.BlockSpec((slot_count, COLS), lambda i, core: (0, i)),
        columns,
        columns,
    ]
    out_specs = [columns, columns]
    out_shape = [jax.ShapeDtypeStruct((tokens, width), jnp.bfloat16)] * 2
    args = [packed, fetched, gate, grad]
    aliases = {}
    if own:
        weight, slot, layer_out, gate_grad, score = last
        picks = weight.shape[1]
        slot = jnp.pad(slot, ((0, 0), (0, LANES - picks)))
        args += [weight, slot, score, layer_out, gate_grad]
        in_specs += [pl.BlockSpec(one.shape, whole) for one in (weight, slot, score)]
        in_specs += [pl.BlockSpec(memory_space=pl.ANY)] * 2
        out_specs.append(pl.BlockSpec((picks, tokens), whole))
        out_shape.append(jax.ShapeDtypeStruct((picks, tokens), jnp.float32))
        aliases = {8: 0, 9: 1}
    else:
        out_specs.append(pl.BlockSpec((tokens, slot_count), whole))
        out_shape.append(jax.ShapeDtypeStruct((tokens, slot_count), jnp.float32))
    return pl.pallas_call(
        functools.partial(read_kernel, own),
        grid_spec=pltpu.PrefetchScalarGridSpec(
            num_scalar_prefetch=1,
            grid=(steps,),
            in_specs=in_specs,
            out_specs=out_specs,
            scratch_shapes=[
                pltpu.VMEM((slot_count, COLS), jnp.bfloat16),
                pltpu.VMEM((tokens, slot_count), jnp.float32),
            ],
        ),
        out_shape=out_shape,
        input_output_aliases=aliases,
        compiler_params=pltpu.CompilerParams(vmem_limit_bytes=VMEM_BYTES),
        cost_estimate=pl.CostEstimate(
            flops=2 * tokens * slot_count * width, bytes_accessed=9 * 2**20, transcendentals=tokens * width // 2
        ),
        name="read_and_scores",
    )(core, *args)


def place_of(core, shifted):
    spot = [(one - core) % RING for one in shifted]
    return (spot[0] * RING + spot[1]) * RING + spot[2]


def shifted_of(core, index):
    return [(one + core) % RING for one in (index // RING**2, index // RING % RING, index % RING)]


def swap(x, axis, crossing=0):
    pairs = []
    for core in range(2):
        for index in range(RING**3):
            shifted = shifted_of(core, index)
            shifted[axis] = ((shifted[axis] + crossing) ^ 1) - crossing
            pairs.append((core * RING**3 + index, core * RING**3 + place_of(core, shifted)))
    return lax.ppermute(x, ("batch", "table"), pairs)


def swap_cores(x):
    return lax.ppermute(x, "batch", [(0, 1), (1, 0)])


def cube_exchange(x):
    groups = []
    for core in range(2):
        found = {}
        for index in range(RING**3):
            shifted = shifted_of(core, index)
            group = tuple((one + 1) % RING // 2 for one in shifted)
            order = sum(bit * (one // 2) for bit, one in zip(BITS, shifted))
            found.setdefault(group, {})[order] = core * RING**3 + index
        groups += [[members[n] for n in range(CUBE)] for _, members in sorted(found.items())]
    return lax.all_to_all(
        x, ("batch", "table"), split_axis=0, concat_axis=0, axis_index_groups=groups, tiled=True
    )


def after(first, then):
    count = len(first)
    return lax.optimization_barrier((*first, *then))[count:]


def local(
    gate_pre, pick_logits, requests, slot_of_pick, values, first_moment, second_moment, out_grad
):
    capacity, table_size = requests.shape
    slot_count = capacity * table_size
    row_count, width = values.shape
    half_width = width // 2
    core = lax.axis_index("batch")
    shifted = shifted_of(core, lax.axis_index("table"))
    inside = sum(bit * (one % 2) for bit, one in zip(BITS, shifted))
    spot = inside.astype(jnp.int32).reshape(1)
    which = core.astype(jnp.int32).reshape(1)

    mine = lax.dynamic_slice(values, (0, core * half_width), (row_count, half_width))
    parts = [mine[:, chunk * CHUNK : (chunk + 1) * CHUNK] for chunk in range(len(ORDERS))]
    swapped = [swap(part, order[0]) for part, order in zip(parts, ORDERS)]

    lists = jnp.stack([requests, swap_cores(requests)]).reshape(2, capacity, RING, RING, RING)
    for axis in range(2, 5):
        turned = jnp.concatenate(
            [lax.slice_in_dim(lists, RING - 1, RING, axis=axis), lax.slice_in_dim(lists, 0, RING - 1, axis=axis)],
            axis=axis,
        )
        lists = jnp.where(core == 0, lists, turned)
    lists = lists.reshape(2, capacity, 2, 2, 2, 2, 2, 2).transpose(2, 4, 6, 0, 3, 5, 7, 1)
    lists = lists.reshape(2 * CUBE, ROW_BLOCK).astype(jnp.float32)

    lists = lists[None]
    crossed = swap(lists, 0, 1)
    gated, gated_theirs = gated_call(which, gate_pre, out_grad)
    gated_other = swap_cores(gated_theirs)
    crossed, *swapped = after([gated], [crossed, *swapped])
    lists = jnp.concatenate([lists, crossed], axis=0)
    crossed = swap(lists, 1, 1)
    parts = [jnp.concatenate(pair, axis=0) for pair in zip(parts, swapped)]
    swapped = [swap(part, order[1]) for part, order in zip(parts, ORDERS)]
    slot = (slot_of_pick % table_size) * capacity + slot_of_pick // table_size
    (slot,) = after(parts, [slot])
    packed, weight = pack_call(pick_logits, slot, slot_count)
    packed_other = swap_cores(packed)
    (crossed,) = after([packed], [crossed])
    lists = jnp.concatenate([lists, crossed], axis=0)
    crossed = swap(lists, 2, 1)
    slot_grad = slot_grad_call(which, packed, packed_other, gated, gated_other)
    crossed, *swapped = after([slot_grad], [crossed, *swapped])
    lists = jnp.concatenate([lists, crossed], axis=0)
    (slot_grad,) = after(swapped, [slot_grad])
    arrived = cube_exchange(slot_grad)
    parts = [jnp.concatenate(pair, axis=0) for pair in zip(parts, swapped)]
    swapped = [swap(part, order[2]) for part, order in zip(parts, ORDERS)]
    gathered = [half for pair in zip(parts, swapped) for half in pair]
    own_cube = sum(bit * (one // 2) for bit, one in zip(BITS, shifted))
    lists = lists.reshape(CUBE, CUBE, 2, ROW_BLOCK)
    lists = lax.dynamic_slice(lists, (0, own_cube, 0, 0), (CUBE, 1, 2, ROW_BLOCK))
    lists = lists.reshape(2, 2, 2, 2, ROW_BLOCK).transpose(2, 1, 0, 3, 4)
    for axis in range(3):
        lists = jnp.where(shifted[axis] // 2 == 0, lists, jnp.flip(lists, axis))
    ids = spread_call(lists.reshape(2 * CUBE, ROW_BLOCK))
    found_other = select_call(1, spot, ids, gathered, half_width)
    found = select_call(0, spot, ids, gathered, half_width)
    (arrived,) = after([found, found_other], [arrived])
    (found_other,) = after([arrived], [found_other])
    fetched_theirs = cube_exchange(found_other)
    halves = [partial_call(chunk, spot, ids, arrived, row_count) for chunk in range(len(ORDERS))]
    received = [swap(send, order[2]) for (_, send), order in zip(halves, ORDERS)]
    (fetched_theirs,) = after(received, [fetched_theirs])
    (found,) = after([fetched_theirs], [found])
    fetched = cube_exchange(found)
    fetched_other = swap_cores(fetched_theirs)

    half = CUBE // 4 * row_count
    for step in (1, 0):
        totals = [keep + other.astype(jnp.float32) for (keep, _), other in zip(halves, received)]
        halves = [(total[:half], total[half:].astype(jnp.bfloat16)) for total in totals]
        received = [swap(send, order[step]) for (_, send), order in zip(halves, ORDERS)]
        half //= 2
    (fetched_other,) = after([send for _, send in halves], [fetched_other])
    layer_out, gate_grad, score = read_call(which, packed, fetched_other, gate_pre, out_grad)
    received = after([score], received)
    totals = [keep + other.astype(jnp.float32) for (keep, _), other in zip(halves, received)]
    own = jnp.concatenate(totals, axis=1)
    value_next, first_next, second_next = adam_call(
        which, own, swap_cores(own), values, first_moment, second_moment
    )
    (fetched,) = after([value_next], [fetched])
    layer_out, gate_grad, logit_grad = read_call(
        which, packed, fetched, gate_pre, out_grad, (weight, slot, layer_out, gate_grad, score)
    )
    return (layer_out, gate_grad, logit_grad.T, value_next, first_next, second_next)


def solution(mesh):
    tokens = P(("batch", "table"), None)
    rows = P("table", None)
    return jax.shard_map(
        local,
        mesh=mesh,
        in_specs=(tokens, tokens, tokens, tokens, rows, rows, rows, tokens),
        out_specs=(tokens, tokens, tokens, rows, rows, rows),
        check_vma=False,
    )
```

```python
import functools

import jax
import jax.numpy as jnp
from jax import lax
from jax.experimental import pallas as pl
from jax.experimental.pallas import tpu as pltpu
from jax.sharding import PartitionSpec as P

learn_rate = 0.001
LANES = 128
COLS = 512
RING = 4
CAPACITY = 16
CUBE = 8
BITS = (4, 2, 1)
ORDERS = ((0, 1, 2), (1, 2, 0), (2, 0, 1))
VMEM_BYTES = 60 * 1024 * 1024


WIDTH = 4096
CHUNK = 768
ROW_BLOCK = LANES


def chunk_width(chunk, total):
    return min(CHUNK, total - chunk * CHUNK)


def slot_place(owner, shift):
    spot = (owner // RING**2, owner // RING % RING, owner % RING)
    places = []
    for core in range(2):
        shifted = [(one + core) % RING for one in spot]
        cube = sum(bit * (one // 2) for bit, one in zip(BITS, shifted))
        chip = sum(bit * (one % 2) for bit, one in zip(BITS, shifted))
        places.append((cube, chip))
    (cube_0, chip_0), (cube_1, chip_1) = places
    cube = cube_0 + shift * (cube_1 - cube_0)
    chip = chip_0 + shift * (chip_1 - chip_0)
    return cube, chip


def pack_kernel(logit_ref, slot_ref, packed_ref, weight_ref):
    tokens, picks = logit_ref.shape
    slot_count = packed_ref.shape[1]
    logits = logit_ref[...]
    raised = jnp.exp(logits - jnp.max(logits, axis=-1, keepdims=True))
    weight_ref[...] = raised / jnp.sum(raised, axis=-1, keepdims=True)
    rows = 16

    @pl.loop(0, tokens // rows)
    def _(step):
        here = pl.ds(pl.multiple_of(step * rows, rows), rows)
        weight = weight_ref[here, :]
        slot = slot_ref[here, :]
        lane = lax.broadcasted_iota(jnp.int32, (rows, slot_count), 1)
        total = jnp.zeros((rows, slot_count), jnp.float32)
        for k in range(picks):
            total = jnp.where(lane == slot[:, k : k + 1], weight[:, k : k + 1], total)
        packed_ref[here, :] = total.astype(jnp.bfloat16)


def pack_call(logits, slot, slot_count):
    tokens, picks = logits.shape
    return pl.pallas_call(
        pack_kernel,
        out_shape=[
            jax.ShapeDtypeStruct((tokens, slot_count), jnp.bfloat16),
            jax.ShapeDtypeStruct((tokens, picks), jnp.float32),
        ],
        compiler_params=pltpu.CompilerParams(vmem_limit_bytes=VMEM_BYTES),
        cost_estimate=pl.CostEstimate(
            flops=2**25, bytes_accessed=2**20, transcendentals=tokens * picks
        ),
        name="pack_weights",
    )(logits, slot)


def gated_kernel(core_ref, gate_a, grad_a, gate_b, grad_b, mine_ref, theirs_ref):
    for gate_ref, grad_ref, out_ref in ((gate_a, grad_a, mine_ref), (gate_b, grad_b, theirs_ref)):
        gate = gate_ref[...].astype(jnp.float32)
        silu = gate * jax.nn.sigmoid(gate)
        out_ref[...] = (grad_ref[...].astype(jnp.float32) * silu).astype(jnp.bfloat16)


def gated_call(core, gate, grad):
    tokens, width = gate.shape
    steps = width // 2 // COLS
    mine = pl.BlockSpec((tokens, COLS), lambda i, core: (0, core[0] * steps + i))
    theirs = pl.BlockSpec((tokens, COLS), lambda i, core: (0, (1 - core[0]) * steps + i))
    half = pl.BlockSpec((tokens, COLS), lambda i, core: (0, i))
    return pl.pallas_call(
        gated_kernel,
        grid_spec=pltpu.PrefetchScalarGridSpec(
            num_scalar_prefetch=1,
            grid=(steps,),
            in_specs=[mine, mine, theirs, theirs],
            out_specs=[half, half],
        ),
        out_shape=[jax.ShapeDtypeStruct((tokens, width // 2), jnp.bfloat16)] * 2,
        compiler_params=pltpu.CompilerParams(vmem_limit_bytes=VMEM_BYTES),
        cost_estimate=pl.CostEstimate(
            flops=4 * tokens * width, bytes_accessed=6 * tokens * width, transcendentals=tokens * width
        ),
        name="gated_halves",
    )(core, gate, grad, gate, grad)


def slot_grad_kernel(
    core_ref, list_ref, packed_ref, packed_other_ref, gated_ref, gated_other_ref, slot_grad_ref
):
    owners = packed_ref.shape[1] // CAPACITY
    groups = ((packed_ref, gated_ref), (packed_other_ref, gated_other_ref))
    for group, (weights, gated) in enumerate(groups):
        found = lax.dot_general(
            weights[...], gated[...], (((0,), (0,)), ((), ())), preferred_element_type=jnp.float32
        ).astype(jnp.bfloat16)
        for owner in range(owners):
            cube, chip = slot_place(owner, core_ref[0])
            start = (cube * 2 + group) * ROW_BLOCK + chip * CAPACITY
            slot_grad_ref[pl.ds(pl.multiple_of(start, CAPACITY), CAPACITY), :] = found[
                owner * CAPACITY : (owner + 1) * CAPACITY, :
            ]

    @pl.when(pl.program_id(0) == pl.num_programs(0) - 1)
    def _():
        ones = jnp.ones((LANES, LANES), jnp.bfloat16)
        row = lax.broadcasted_iota(jnp.int32, (LANES, LANES), 0)
        lane = lax.broadcasted_iota(jnp.int32, (LANES, LANES), 1)
        start = WIDTH // 2 - (len(ORDERS) - 1) * CHUNK
        for block in range(list_ref.shape[0]):
            diagonal = jnp.where(row == lane, list_ref[block : block + 1, :], 0.0)
            slot_grad_ref[block * LANES : (block + 1) * LANES, start : start + LANES] = jnp.dot(
                diagonal.astype(jnp.bfloat16), ones, preferred_element_type=jnp.float32
            ).astype(jnp.bfloat16)


def slot_grad_call(core, lists, packed, packed_other, gated, gated_other):
    tokens, half = gated.shape
    slot_count = packed.shape[1]
    whole = lambda i: (0, 0)
    by_cols = lambda i: (0, i)
    weights = pl.BlockSpec((tokens, slot_count), whole)
    columns = pl.BlockSpec((tokens, CHUNK), by_cols)
    return pl.pallas_call(
        slot_grad_kernel,
        grid=(len(ORDERS),),
        in_specs=[
            pl.BlockSpec(memory_space=pltpu.SMEM),
            pl.BlockSpec(lists.shape, whole),
            weights, weights, columns, columns,
        ],
        out_specs=pl.BlockSpec((2 * slot_count, CHUNK), by_cols),
        out_shape=jax.ShapeDtypeStruct((2 * slot_count, half + LANES), jnp.bfloat16),
        compiler_params=pltpu.CompilerParams(vmem_limit_bytes=VMEM_BYTES),
        cost_estimate=pl.CostEstimate(
            flops=4 * tokens * slot_count * half, bytes_accessed=14 * 2**20, transcendentals=0
        ),
        name="slot_gradients",
    )(core, lists, packed, packed_other, gated, gated_other)


def relative(order, position):
    return sum(BITS[axis] for bit, axis in enumerate(order) if position >> bit & 1)


def asked_at(owner, peer, group):
    start = (peer * 2 + group) * ROW_BLOCK + owner * CAPACITY
    return pl.ds(pl.multiple_of(start, CAPACITY), CAPACITY)


def asked_rows(ref, owner, groups):
    return jnp.concatenate(
        [ref[asked_at(owner, peer, group), :] for peer in range(CUBE) for group in groups], axis=0
    )


def chosen_rows(id_ref, owner, groups):
    ids = asked_rows(id_ref, owner, groups)
    lane = lax.broadcasted_iota(jnp.int32, ids.shape, 1)
    return (ids.astype(jnp.float32) == lane.astype(jnp.float32)).astype(jnp.bfloat16)


def select_kernel(group, spot_ref, id_ref, *refs):
    out_ref = refs[-1]
    for chunk, order in enumerate(ORDERS):
        near, far = refs[2 * chunk], refs[2 * chunk + 1]
        rows = near.shape[0] * 2 // CUBE

        @pl.when(pl.program_id(0) == chunk)
        def _(order=order, near=near, far=far, rows=rows):
            for position in range(CUBE):
                source = near if position < CUBE // 2 else far
                start = position % (CUBE // 2) * rows
                owner = spot_ref[0] ^ relative(order, position)
                found = jnp.dot(
                    chosen_rows(id_ref, owner, (group,)),
                    source[start : start + rows, :],
                    preferred_element_type=jnp.float32,
                ).astype(jnp.bfloat16)
                for peer in range(CUBE):
                    at = pl.ds(
                        pl.multiple_of(peer * ROW_BLOCK + owner * CAPACITY, CAPACITY), CAPACITY
                    )
                    out_ref[at, : found.shape[1]] = found[peer * CAPACITY : (peer + 1) * CAPACITY, :]


def select_call(group, spot, arrived, parts):
    rows, wide = arrived.shape
    whole = lambda i: (0, 0)
    return pl.pallas_call(
        functools.partial(select_kernel, group),
        grid=(len(ORDERS),),
        in_specs=[
            pl.BlockSpec(memory_space=pltpu.SMEM),
            pl.BlockSpec((rows, LANES), lambda i: (0, wide // LANES - 1)),
        ]
        + [pl.BlockSpec(part.shape, whole) for part in parts],
        out_specs=pl.BlockSpec((rows // 2, CHUNK), lambda i: (0, i)),
        out_shape=jax.ShapeDtypeStruct((rows // 2, wide - LANES), jnp.bfloat16),
        compiler_params=pltpu.CompilerParams(vmem_limit_bytes=VMEM_BYTES),
        cost_estimate=pl.CostEstimate(
            flops=rows * LANES * wide, bytes_accessed=3 * rows * wide, transcendentals=0
        ),
        name="select_rows",
    )(spot, arrived, *parts)


def partial_kernel(chunk, spot_ref, id_ref, arrived_ref, keep_ref, send_ref):
    rows = keep_ref.shape[0] * 2 // CUBE
    cols = keep_ref.shape[1]
    for position in range(CUBE):
        owner = spot_ref[0] ^ relative(ORDERS[chunk], position)
        chosen = chosen_rows(id_ref, owner, (0, 1))
        by_rows = (((0,), (0,)), ((), ()))
        total = lax.dot_general(
            chosen, asked_rows(arrived_ref, owner, (0, 1))[:, :cols], by_rows,
            preferred_element_type=jnp.float32,
        )
        target = keep_ref if position < CUBE // 2 else send_ref
        start = position % (CUBE // 2) * rows
        target[start : start + rows, :] = total.astype(target.dtype)
        if chunk == len(ORDERS) - 1:
            hits = lax.dot_general(
                chosen, jnp.ones(chosen.shape, jnp.bfloat16), by_rows, preferred_element_type=jnp.float32
            )
            target[start : start + rows, cols - LANES :] = hits.astype(target.dtype)


def partial_call(chunk, spot, arrived, row_count):
    rows, wide = arrived.shape
    cols = chunk_width(chunk, wide)
    half = CUBE // 2 * row_count
    whole = lambda i: (0, 0)
    return pl.pallas_call(
        functools.partial(partial_kernel, chunk),
        grid=(1,),
        in_specs=[
            pl.BlockSpec(memory_space=pltpu.SMEM),
            pl.BlockSpec((rows, LANES), lambda i: (0, wide // LANES - 1)),
            pl.BlockSpec((rows, CHUNK), lambda i: (0, chunk)),
        ],
        out_specs=[pl.BlockSpec((half, cols), whole)] * 2,
        out_shape=[
            jax.ShapeDtypeStruct((half, cols), jnp.float32),
            jax.ShapeDtypeStruct((half, cols), jnp.bfloat16),
        ],
        compiler_params=pltpu.CompilerParams(vmem_limit_bytes=VMEM_BYTES),
        cost_estimate=pl.CostEstimate(
            flops=2 * rows * LANES * cols, bytes_accessed=8 * rows * cols, transcendentals=0
        ),
        name="partial_sums",
    )(spot, arrived, arrived)


def adam_kernel(
    core_ref, hits_ref, own_ref, other_ref, value_ref, first_ref, second_ref,
    value_out, first_out, second_out,
):
    touched = hits_ref[...][:, :1] > 0.0
    own = pl.program_id(0) < pl.num_programs(0) // 2
    row_grad = jnp.where(own, own_ref[...], other_ref[...])
    first = first_ref[...]
    second = second_ref[...]
    value = value_ref[...].astype(jnp.float32)
    first_new = 0.9 * first + 0.1 * row_grad
    second_new = 0.95 * second + 0.05 * row_grad * row_grad
    value_new = value - learn_rate * first_new / (jnp.sqrt(second_new) + 1e-08)
    value_out[...] = jnp.where(touched, value_new, value).astype(jnp.bfloat16)
    first_out[...] = jnp.where(touched, first_new, first)
    second_out[...] = jnp.where(touched, second_new, second)


def adam_call(core, own, other, values, first, second):
    rows, width = values.shape
    steps = width // 2 // COLS
    columns = pl.BlockSpec(
        (rows, COLS),
        lambda i, core: (0, lax.rem(core[0] + i // steps, 2) * steps + lax.rem(i, steps)),
    )
    return pl.pallas_call(
        adam_kernel,
        grid_spec=pltpu.PrefetchScalarGridSpec(
            num_scalar_prefetch=1,
            grid=(2 * steps,),
            in_specs=[
                pl.BlockSpec((rows, LANES), lambda i, core: (0, width // 2 // LANES)),
                pl.BlockSpec((rows, COLS), lambda i, core: (0, jnp.minimum(i, steps - 1))),
                pl.BlockSpec((rows, COLS), lambda i, core: (0, jnp.maximum(i - steps, 0))),
                columns, columns, columns,
            ],
            out_specs=[columns] * 3,
        ),
        out_shape=[
            jax.ShapeDtypeStruct(values.shape, values.dtype),
            jax.ShapeDtypeStruct(first.shape, first.dtype),
            jax.ShapeDtypeStruct(second.shape, second.dtype),
        ],
        compiler_params=pltpu.CompilerParams(vmem_limit_bytes=VMEM_BYTES),
        cost_estimate=pl.CostEstimate(
            flops=10 * rows * width, bytes_accessed=28 * rows * width, transcendentals=rows * width
        ),
        name="adam_rows",
    )(core, own, own, other, values, first, second)


def read_kernel(own, core_ref, packed_ref, fetched_ref, gate_ref, grad_ref, *refs):
    if own:
        weight_ref, slot_ref, before_ref, _, _, out_ref, gate_grad_ref, logit_grad_ref = refs[:8]
    else:
        out_ref, gate_grad_ref, score_out_ref = refs[:3]
    ordered_ref, score_ref = refs[-2:]
    step = pl.program_id(0)
    shift = core_ref[0] if own else 1 - core_ref[0]
    for owner in range(ordered_ref.shape[0] // CAPACITY):
        cube, chip = slot_place(owner, shift)
        at = pl.ds(pl.multiple_of(cube * ROW_BLOCK + chip * CAPACITY, CAPACITY), CAPACITY)
        ordered_ref[owner * CAPACITY : (owner + 1) * CAPACITY, :] = fetched_ref[at, :]
    fetched = ordered_ref[...]
    memory = jnp.dot(packed_ref[...], fetched, preferred_element_type=jnp.float32)
    gate = gate_ref[...].astype(jnp.float32)
    sig = jax.nn.sigmoid(gate)
    silu = gate * sig
    grad = grad_ref[...].astype(jnp.float32)
    out_ref[...] = (silu * memory).astype(jnp.bfloat16)
    gated = (grad * silu).astype(jnp.bfloat16)
    gate_grad_ref[...] = (grad * memory * sig * (1.0 + gate * (1.0 - sig))).astype(jnp.bfloat16)
    score = lax.dot_general(
        gated, fetched, (((1,), (1,)), ((), ())), preferred_element_type=jnp.float32
    )

    @pl.when(step == 0)
    def _():
        score_ref[...] = score + before_ref[...] if own else score

    @pl.when(step > 0)
    def _():
        score_ref[...] += score

    @pl.when(step == pl.num_programs(0) - 1)
    def _():
        if not own:
            score_out_ref[...] = score_ref[...]
            return
        picks = weight_ref.shape[1]
        slot = slot_ref[...]
        low = lax.rem(slot, LANES)
        high = slot // LANES
        wide = jnp.zeros(slot.shape, jnp.float32)
        for part in range(score_ref.shape[1] // LANES):
            here = score_ref[:, part * LANES : (part + 1) * LANES]
            wide = jnp.where(high == part, jnp.take_along_axis(here, low, axis=1), wide)
        pick_score = wide[:, :picks]
        weight = weight_ref[...]
        mean_score = jnp.sum(weight * pick_score, axis=-1, keepdims=True)
        wide = jnp.pad(weight * (pick_score - mean_score), ((0, 0), (0, LANES - picks)))
        logit_grad_ref[...] = wide.T[:picks, :]


def read_call(core, packed, fetched, gate, grad, last=None):
    tokens, width = gate.shape
    slot_count = packed.shape[1]
    steps = width // 2 // COLS
    own = last is not None
    whole = lambda i, core: (0, 0)

    def by_cols(i, core):
        half = core[0] if own else 1 - core[0]
        return (0, half * steps + i)

    columns = pl.BlockSpec((tokens, COLS), by_cols)
    in_specs = [
        pl.BlockSpec((tokens, slot_count), whole),
        pl.BlockSpec((slot_count, COLS), lambda i, core: (0, i)),
        columns,
        columns,
    ]
    out_specs = [columns, columns]
    out_shape = [jax.ShapeDtypeStruct((tokens, width), jnp.bfloat16)] * 2
    args = [packed, fetched, gate, grad]
    aliases = {}
    if own:
        weight, slot, layer_out, gate_grad, score = last
        picks = weight.shape[1]
        slot = jnp.pad(slot, ((0, 0), (0, LANES - picks)))
        args += [weight, slot, score, layer_out, gate_grad]
        in_specs += [pl.BlockSpec(one.shape, whole) for one in (weight, slot, score)]
        in_specs += [pl.BlockSpec(memory_space=pl.ANY)] * 2
        out_specs.append(pl.BlockSpec((picks, tokens), whole))
        out_shape.append(jax.ShapeDtypeStruct((picks, tokens), jnp.float32))
        aliases = {8: 0, 9: 1}
    else:
        out_specs.append(pl.BlockSpec((tokens, slot_count), whole))
        out_shape.append(jax.ShapeDtypeStruct((tokens, slot_count), jnp.float32))
    return pl.pallas_call(
        functools.partial(read_kernel, own),
        grid_spec=pltpu.PrefetchScalarGridSpec(
            num_scalar_prefetch=1,
            grid=(steps,),
            in_specs=in_specs,
            out_specs=out_specs,
            scratch_shapes=[
                pltpu.VMEM((slot_count, COLS), jnp.bfloat16),
                pltpu.VMEM((tokens, slot_count), jnp.float32),
            ],
        ),
        out_shape=out_shape,
        input_output_aliases=aliases,
        compiler_params=pltpu.CompilerParams(vmem_limit_bytes=VMEM_BYTES),
        cost_estimate=pl.CostEstimate(
            flops=2 * tokens * slot_count * width, bytes_accessed=9 * 2**20, transcendentals=tokens * width // 2
        ),
        name="read_and_scores",
    )(core, *args)


def place_of(core, shifted):
    spot = [(one - core) % RING for one in shifted]
    return (spot[0] * RING + spot[1]) * RING + spot[2]


def shifted_of(core, index):
    return [(one + core) % RING for one in (index // RING**2, index // RING % RING, index % RING)]


def swap(x, axis):
    pairs = []
    for core in range(2):
        for index in range(RING**3):
            shifted = shifted_of(core, index)
            shifted[axis] ^= 1
            pairs.append((core * RING**3 + index, core * RING**3 + place_of(core, shifted)))
    return lax.ppermute(x, ("batch", "table"), pairs)


def swap_cores(x):
    return lax.ppermute(x, "batch", [(0, 1), (1, 0)])


def cube_exchange(x):
    groups = []
    for core in range(2):
        found = {}
        for index in range(RING**3):
            shifted = shifted_of(core, index)
            group = tuple((one + 1) % RING // 2 for one in shifted)
            order = sum(bit * (one // 2) for bit, one in zip(BITS, shifted))
            found.setdefault(group, {})[order] = core * RING**3 + index
        groups += [[members[n] for n in range(CUBE)] for _, members in sorted(found.items())]
    return lax.all_to_all(
        x, ("batch", "table"), split_axis=0, concat_axis=0, axis_index_groups=groups, tiled=True
    )


def after(first, then):
    count = len(first)
    return lax.optimization_barrier((*first, *then))[count:]


def local(
    gate_pre, pick_logits, requests, slot_of_pick, values, first_moment, second_moment, out_grad
):
    capacity, table_size = requests.shape
    slot_count = capacity * table_size
    row_count, width = values.shape
    half_width = width // 2
    core = lax.axis_index("batch")
    shifted = shifted_of(core, lax.axis_index("table"))
    inside = sum(bit * (one % 2) for bit, one in zip(BITS, shifted))
    spot = inside.astype(jnp.int32).reshape(1)
    which = core.astype(jnp.int32).reshape(1)

    mine = lax.dynamic_slice(values, (0, core * half_width), (row_count, half_width))
    parts = [mine[:, chunk * CHUNK : (chunk + 1) * CHUNK] for chunk in range(len(ORDERS))]
    swapped = [swap(part, order[0]) for part, order in zip(parts, ORDERS)]

    lists = jnp.stack([requests, swap_cores(requests)]).reshape(2, capacity, RING, RING, RING)
    for axis in range(2, 5):
        turned = jnp.concatenate(
            [lax.slice_in_dim(lists, RING - 1, RING, axis=axis), lax.slice_in_dim(lists, 0, RING - 1, axis=axis)],
            axis=axis,
        )
        lists = jnp.where(core == 0, lists, turned)
    lists = lists.reshape(2, capacity, 2, 2, 2, 2, 2, 2).transpose(2, 4, 6, 0, 3, 5, 7, 1)
    lists = lists.reshape(2 * CUBE, ROW_BLOCK).astype(jnp.float32)

    gated, gated_theirs = gated_call(which, gate_pre, out_grad)
    gated_other = swap_cores(gated_theirs)
    swapped = after([gated], swapped)
    parts = [jnp.concatenate(pair, axis=0) for pair in zip(parts, swapped)]
    swapped = [swap(part, order[1]) for part, order in zip(parts, ORDERS)]
    slot = (slot_of_pick % table_size) * capacity + slot_of_pick // table_size
    (slot,) = after(parts, [slot])
    packed, weight = pack_call(pick_logits, slot, slot_count)
    packed_other = swap_cores(packed)
    slot_grad = slot_grad_call(which, lists, packed, packed_other, gated, gated_other)
    swapped = after([slot_grad], swapped)
    (slot_grad,) = after(swapped, [slot_grad])
    arrived = cube_exchange(slot_grad)
    parts = [jnp.concatenate(pair, axis=0) for pair in zip(parts, swapped)]
    swapped = [swap(part, order[2]) for part, order in zip(parts, ORDERS)]
    gathered = [half for pair in zip(parts, swapped) for half in pair]
    (arrived,) = after(swapped, [arrived])

    found_other = select_call(1, spot, arrived, gathered)
    fetched_theirs = cube_exchange(found_other)
    (arrived,) = after([found_other], [arrived])
    halves = [partial_call(chunk, spot, arrived, row_count) for chunk in range(len(ORDERS))]
    (arrived,) = after([keep for keep, _ in halves], [arrived])
    found = select_call(0, spot, arrived, gathered)
    received = [swap(send, order[2]) for (_, send), order in zip(halves, ORDERS)]
    received = after([found], received)
    half = CUBE // 4 * row_count
    totals = [keep + other.astype(jnp.float32) for (keep, _), other in zip(halves, received)]
    halves = [(total[:half], total[half:].astype(jnp.bfloat16)) for total in totals]
    received = [swap(send, order[1]) for (_, send), order in zip(halves, ORDERS)]
    (found,) = after([fetched_theirs, *received], [found])
    fetched = cube_exchange(found)
    fetched_other = swap_cores(fetched_theirs)

    half //= 2
    totals = [keep + other.astype(jnp.float32) for (keep, _), other in zip(halves, received)]
    halves = [(total[:half], total[half:].astype(jnp.bfloat16)) for total in totals]
    received = [swap(send, order[0]) for (_, send), order in zip(halves, ORDERS)]
    layer_out, gate_grad, score = read_call(which, packed, fetched_other, gate_pre, out_grad)
    received = after([score], received)
    totals = [keep + other.astype(jnp.float32) for (keep, _), other in zip(halves, received)]
    own = jnp.concatenate(totals, axis=1)
    value_next, first_next, second_next = adam_call(
        which, own, swap_cores(own), values, first_moment, second_moment
    )
    (fetched,) = after([value_next], [fetched])
    layer_out, gate_grad, logit_grad = read_call(
        which, packed, fetched, gate_pre, out_grad, (weight, slot, layer_out, gate_grad, score)
    )
    return (layer_out, gate_grad, logit_grad.T, value_next, first_next, second_next)


def solution(mesh):
    tokens = P(("batch", "table"), None)
    rows = P("table", None)
    return jax.shard_map(
        local,
        mesh=mesh,
        in_specs=(tokens, tokens, tokens, tokens, rows, rows, rows, tokens),
        out_specs=(tokens, tokens, tokens, rows, rows, rows),
        check_vma=False,
    )
```

```python
import functools

import jax
import jax.numpy as jnp
from jax import lax
from jax.experimental import pallas as pl
from jax.experimental.pallas import tpu as pltpu
from jax.sharding import PartitionSpec as P

learn_rate = 0.001
LANES = 128
COLS = 512
RING = 4
CAPACITY = 16
CUBE = 8
BITS = (4, 2, 1)
ORDERS = ((0, 1, 2), (1, 2, 0), (2, 0, 1))
VMEM_BYTES = 60 * 1024 * 1024


WIDTH = 4096
CHUNK = 768
ROW_BLOCK = LANES


def chunk_width(chunk, total):
    return min(CHUNK, total - chunk * CHUNK)


def slot_place(owner, shift):
    spot = (owner // RING**2, owner // RING % RING, owner % RING)
    places = []
    for core in range(2):
        shifted = [(one + core) % RING for one in spot]
        cube = sum(bit * (one // 2) for bit, one in zip(BITS, shifted))
        chip = sum(bit * (one % 2) for bit, one in zip(BITS, shifted))
        places.append((cube, chip))
    (cube_0, chip_0), (cube_1, chip_1) = places
    cube = cube_0 + shift * (cube_1 - cube_0)
    chip = chip_0 + shift * (chip_1 - chip_0)
    return cube, chip


def pack_kernel(logit_ref, slot_ref, packed_ref, weight_ref):
    tokens, picks = logit_ref.shape
    slot_count = packed_ref.shape[1]
    logits = logit_ref[...]
    raised = jnp.exp(logits - jnp.max(logits, axis=-1, keepdims=True))
    weight_ref[...] = raised / jnp.sum(raised, axis=-1, keepdims=True)
    rows = 16

    @pl.loop(0, tokens // rows)
    def _(step):
        here = pl.ds(pl.multiple_of(step * rows, rows), rows)
        weight = weight_ref[here, :]
        slot = slot_ref[here, :]
        lane = lax.broadcasted_iota(jnp.int32, (rows, slot_count), 1)
        total = jnp.zeros((rows, slot_count), jnp.float32)
        for k in range(picks):
            total = jnp.where(lane == slot[:, k : k + 1], weight[:, k : k + 1], total)
        packed_ref[here, :] = total.astype(jnp.bfloat16)


def pack_call(logits, slot, slot_count):
    tokens, picks = logits.shape
    return pl.pallas_call(
        pack_kernel,
        out_shape=[
            jax.ShapeDtypeStruct((tokens, slot_count), jnp.bfloat16),
            jax.ShapeDtypeStruct((tokens, picks), jnp.float32),
        ],
        compiler_params=pltpu.CompilerParams(vmem_limit_bytes=VMEM_BYTES),
        cost_estimate=pl.CostEstimate(
            flops=2**25, bytes_accessed=2**20, transcendentals=tokens * picks
        ),
        name="pack_weights",
    )(logits, slot)


def gated_kernel(core_ref, gate_a, grad_a, gate_b, grad_b, mine_ref, theirs_ref):
    for gate_ref, grad_ref, out_ref in ((gate_a, grad_a, mine_ref), (gate_b, grad_b, theirs_ref)):
        gate = gate_ref[...].astype(jnp.float32)
        silu = gate * jax.nn.sigmoid(gate)
        out_ref[...] = (grad_ref[...].astype(jnp.float32) * silu).astype(jnp.bfloat16)


def gated_call(core, gate, grad):
    tokens, width = gate.shape
    steps = width // 2 // COLS
    mine = pl.BlockSpec((tokens, COLS), lambda i, core: (0, core[0] * steps + i))
    theirs = pl.BlockSpec((tokens, COLS), lambda i, core: (0, (1 - core[0]) * steps + i))
    half = pl.BlockSpec((tokens, COLS), lambda i, core: (0, i))
    return pl.pallas_call(
        gated_kernel,
        grid_spec=pltpu.PrefetchScalarGridSpec(
            num_scalar_prefetch=1,
            grid=(steps,),
            in_specs=[mine, mine, theirs, theirs],
            out_specs=[half, half],
        ),
        out_shape=[jax.ShapeDtypeStruct((tokens, width // 2), jnp.bfloat16)] * 2,
        compiler_params=pltpu.CompilerParams(vmem_limit_bytes=VMEM_BYTES),
        cost_estimate=pl.CostEstimate(
            flops=4 * tokens * width, bytes_accessed=6 * tokens * width, transcendentals=tokens * width
        ),
        name="gated_halves",
    )(core, gate, grad, gate, grad)


def slot_grad_kernel(
    core_ref, list_ref, packed_ref, packed_other_ref, gated_ref, gated_other_ref, slot_grad_ref
):
    owners = packed_ref.shape[1] // CAPACITY
    groups = ((packed_ref, gated_ref), (packed_other_ref, gated_other_ref))
    for group, (weights, gated) in enumerate(groups):
        found = lax.dot_general(
            weights[...], gated[...], (((0,), (0,)), ((), ())), preferred_element_type=jnp.float32
        ).astype(jnp.bfloat16)
        for owner in range(owners):
            cube, chip = slot_place(owner, core_ref[0])
            start = (cube * 2 + group) * ROW_BLOCK + chip * CAPACITY
            slot_grad_ref[pl.ds(pl.multiple_of(start, CAPACITY), CAPACITY), :] = found[
                owner * CAPACITY : (owner + 1) * CAPACITY, :
            ]

    @pl.when(pl.program_id(0) == pl.num_programs(0) - 1)
    def _():
        ones = jnp.ones((LANES, LANES), jnp.bfloat16)
        row = lax.broadcasted_iota(jnp.int32, (LANES, LANES), 0)
        lane = lax.broadcasted_iota(jnp.int32, (LANES, LANES), 1)
        start = WIDTH // 2 - (len(ORDERS) - 1) * CHUNK
        for block in range(list_ref.shape[0]):
            diagonal = jnp.where(row == lane, list_ref[block : block + 1, :], 0.0)
            slot_grad_ref[block * LANES : (block + 1) * LANES, start : start + LANES] = jnp.dot(
                diagonal.astype(jnp.bfloat16), ones, preferred_element_type=jnp.float32
            ).astype(jnp.bfloat16)


def slot_grad_call(core, lists, packed, packed_other, gated, gated_other):
    tokens, half = gated.shape
    slot_count = packed.shape[1]
    whole = lambda i: (0, 0)
    by_cols = lambda i: (0, i)
    weights = pl.BlockSpec((tokens, slot_count), whole)
    columns = pl.BlockSpec((tokens, CHUNK), by_cols)
    return pl.pallas_call(
        slot_grad_kernel,
        grid=(len(ORDERS),),
        in_specs=[
            pl.BlockSpec(memory_space=pltpu.SMEM),
            pl.BlockSpec(lists.shape, whole),
            weights, weights, columns, columns,
        ],
        out_specs=pl.BlockSpec((2 * slot_count, CHUNK), by_cols),
        out_shape=jax.ShapeDtypeStruct((2 * slot_count, half + LANES), jnp.bfloat16),
        compiler_params=pltpu.CompilerParams(vmem_limit_bytes=VMEM_BYTES),
        cost_estimate=pl.CostEstimate(
            flops=4 * tokens * slot_count * half, bytes_accessed=14 * 2**20, transcendentals=0
        ),
        name="slot_gradients",
    )(core, lists, packed, packed_other, gated, gated_other)


def relative(order, position):
    return sum(BITS[axis] for bit, axis in enumerate(order) if position >> bit & 1)


def asked_at(owner, peer, group):
    start = (peer * 2 + group) * ROW_BLOCK + owner * CAPACITY
    return pl.ds(pl.multiple_of(start, CAPACITY), CAPACITY)


def asked_rows(ref, owner, groups):
    return jnp.concatenate(
        [ref[asked_at(owner, peer, group), :] for peer in range(CUBE) for group in groups], axis=0
    )


def chosen_rows(id_ref, owner, groups):
    ids = asked_rows(id_ref, owner, groups)
    lane = lax.broadcasted_iota(jnp.int32, ids.shape, 1)
    return (ids.astype(jnp.float32) == lane.astype(jnp.float32)).astype(jnp.bfloat16)


def select_kernel(group, spot_ref, id_ref, *refs):
    out_ref = refs[-1]
    for chunk, order in enumerate(ORDERS):
        near, far = refs[2 * chunk], refs[2 * chunk + 1]
        rows = near.shape[0] * 2 // CUBE

        @pl.when(pl.program_id(0) == chunk)
        def _(order=order, near=near, far=far, rows=rows):
            for position in range(CUBE):
                source = near if position < CUBE // 2 else far
                start = position % (CUBE // 2) * rows
                owner = spot_ref[0] ^ relative(order, position)
                found = jnp.dot(
                    chosen_rows(id_ref, owner, (group,)),
                    source[start : start + rows, :],
                    preferred_element_type=jnp.float32,
                ).astype(jnp.bfloat16)
                for peer in range(CUBE):
                    at = pl.ds(
                        pl.multiple_of(peer * ROW_BLOCK + owner * CAPACITY, CAPACITY), CAPACITY
                    )
                    out_ref[at, : found.shape[1]] = found[peer * CAPACITY : (peer + 1) * CAPACITY, :]


def select_call(group, spot, arrived, parts):
    rows, wide = arrived.shape
    whole = lambda i: (0, 0)
    return pl.pallas_call(
        functools.partial(select_kernel, group),
        grid=(len(ORDERS),),
        in_specs=[
            pl.BlockSpec(memory_space=pltpu.SMEM),
            pl.BlockSpec((rows, LANES), lambda i: (0, wide // LANES - 1)),
        ]
        + [pl.BlockSpec(part.shape, whole) for part in parts],
        out_specs=pl.BlockSpec((rows // 2, CHUNK), lambda i: (0, i)),
        out_shape=jax.ShapeDtypeStruct((rows // 2, wide - LANES), jnp.bfloat16),
        compiler_params=pltpu.CompilerParams(vmem_limit_bytes=VMEM_BYTES),
        cost_estimate=pl.CostEstimate(
            flops=rows * LANES * wide, bytes_accessed=3 * rows * wide, transcendentals=0
        ),
        name="select_rows",
    )(spot, arrived, *parts)


def partial_kernel(chunk, spot_ref, id_ref, arrived_ref, keep_ref, send_ref):
    rows = keep_ref.shape[0] * 2 // CUBE
    cols = keep_ref.shape[1]
    for position in range(CUBE):
        owner = spot_ref[0] ^ relative(ORDERS[chunk], position)
        chosen = chosen_rows(id_ref, owner, (0, 1))
        by_rows = (((0,), (0,)), ((), ()))
        total = lax.dot_general(
            chosen, asked_rows(arrived_ref, owner, (0, 1))[:, :cols], by_rows,
            preferred_element_type=jnp.float32,
        )
        target = keep_ref if position < CUBE // 2 else send_ref
        start = position % (CUBE // 2) * rows
        target[start : start + rows, :] = total.astype(target.dtype)
        if chunk == len(ORDERS) - 1:
            hits = lax.dot_general(
                chosen, jnp.ones(chosen.shape, jnp.bfloat16), by_rows, preferred_element_type=jnp.float32
            )
            target[start : start + rows, cols - LANES :] = hits.astype(target.dtype)


def partial_call(chunk, spot, arrived, row_count):
    rows, wide = arrived.shape
    cols = chunk_width(chunk, wide)
    half = CUBE // 2 * row_count
    whole = lambda i: (0, 0)
    return pl.pallas_call(
        functools.partial(partial_kernel, chunk),
        grid=(1,),
        in_specs=[
            pl.BlockSpec(memory_space=pltpu.SMEM),
            pl.BlockSpec((rows, LANES), lambda i: (0, wide // LANES - 1)),
            pl.BlockSpec((rows, CHUNK), lambda i: (0, chunk)),
        ],
        out_specs=[pl.BlockSpec((half, cols), whole)] * 2,
        out_shape=[
            jax.ShapeDtypeStruct((half, cols), jnp.float32),
            jax.ShapeDtypeStruct((half, cols), jnp.bfloat16),
        ],
        compiler_params=pltpu.CompilerParams(vmem_limit_bytes=VMEM_BYTES),
        cost_estimate=pl.CostEstimate(
            flops=2 * rows * LANES * cols, bytes_accessed=8 * rows * cols, transcendentals=0
        ),
        name="partial_sums",
    )(spot, arrived, arrived)


def adam_kernel(
    core_ref, hits_ref, own_ref, other_ref, value_ref, first_ref, second_ref,
    value_out, first_out, second_out,
):
    touched = hits_ref[...][:, :1] > 0.0
    own = pl.program_id(0) < pl.num_programs(0) // 2
    row_grad = jnp.where(own, own_ref[...], other_ref[...])
    first = first_ref[...]
    second = second_ref[...]
    value = value_ref[...].astype(jnp.float32)
    first_new = 0.9 * first + 0.1 * row_grad
    second_new = 0.95 * second + 0.05 * row_grad * row_grad
    value_new = value - learn_rate * first_new / (jnp.sqrt(second_new) + 1e-08)
    value_out[...] = jnp.where(touched, value_new, value).astype(jnp.bfloat16)
    first_out[...] = jnp.where(touched, first_new, first)
    second_out[...] = jnp.where(touched, second_new, second)


def adam_call(core, own, other, values, first, second):
    rows, width = values.shape
    steps = width // 2 // COLS
    columns = pl.BlockSpec(
        (rows, COLS),
        lambda i, core: (0, lax.rem(core[0] + i // steps, 2) * steps + lax.rem(i, steps)),
    )
    return pl.pallas_call(
        adam_kernel,
        grid_spec=pltpu.PrefetchScalarGridSpec(
            num_scalar_prefetch=1,
            grid=(2 * steps,),
            in_specs=[
                pl.BlockSpec((rows, LANES), lambda i, core: (0, width // 2 // LANES)),
                pl.BlockSpec((rows, COLS), lambda i, core: (0, jnp.minimum(i, steps - 1))),
                pl.BlockSpec((rows, COLS), lambda i, core: (0, jnp.maximum(i - steps, 0))),
                columns, columns, columns,
            ],
            out_specs=[columns] * 3,
        ),
        out_shape=[
            jax.ShapeDtypeStruct(values.shape, values.dtype),
            jax.ShapeDtypeStruct(first.shape, first.dtype),
            jax.ShapeDtypeStruct(second.shape, second.dtype),
        ],
        compiler_params=pltpu.CompilerParams(vmem_limit_bytes=VMEM_BYTES),
        cost_estimate=pl.CostEstimate(
            flops=10 * rows * width, bytes_accessed=28 * rows * width, transcendentals=rows * width
        ),
        name="adam_rows",
    )(core, own, own, other, values, first, second)


def read_kernel(own, core_ref, packed_ref, fetched_ref, gate_ref, grad_ref, *refs):
    if own:
        weight_ref, slot_ref, before_ref, _, _, out_ref, gate_grad_ref, logit_grad_ref = refs[:8]
    else:
        out_ref, gate_grad_ref, score_out_ref = refs[:3]
    ordered_ref, score_ref = refs[-2:]
    step = pl.program_id(0)
    shift = core_ref[0] if own else 1 - core_ref[0]
    for owner in range(ordered_ref.shape[0] // CAPACITY):
        cube, chip = slot_place(owner, shift)
        at = pl.ds(pl.multiple_of(cube * ROW_BLOCK + chip * CAPACITY, CAPACITY), CAPACITY)
        ordered_ref[owner * CAPACITY : (owner + 1) * CAPACITY, :] = fetched_ref[at, :]
    fetched = ordered_ref[...]
    memory = jnp.dot(packed_ref[...], fetched, preferred_element_type=jnp.float32)
    gate = gate_ref[...].astype(jnp.float32)
    sig = jax.nn.sigmoid(gate)
    silu = gate * sig
    grad = grad_ref[...].astype(jnp.float32)
    out_ref[...] = (silu * memory).astype(jnp.bfloat16)
    gated = (grad * silu).astype(jnp.bfloat16)
    gate_grad_ref[...] = (grad * memory * sig * (1.0 + gate * (1.0 - sig))).astype(jnp.bfloat16)
    score = lax.dot_general(
        gated, fetched, (((1,), (1,)), ((), ())), preferred_element_type=jnp.float32
    )

    @pl.when(step == 0)
    def _():
        score_ref[...] = score + before_ref[...] if own else score

    @pl.when(step > 0)
    def _():
        score_ref[...] += score

    @pl.when(step == pl.num_programs(0) - 1)
    def _():
        if not own:
            score_out_ref[...] = score_ref[...]
            return
        picks = weight_ref.shape[1]
        slot = slot_ref[...]
        low = lax.rem(slot, LANES)
        high = slot // LANES
        wide = jnp.zeros(slot.shape, jnp.float32)
        for part in range(score_ref.shape[1] // LANES):
            here = score_ref[:, part * LANES : (part + 1) * LANES]
            wide = jnp.where(high == part, jnp.take_along_axis(here, low, axis=1), wide)
        pick_score = wide[:, :picks]
        weight = weight_ref[...]
        mean_score = jnp.sum(weight * pick_score, axis=-1, keepdims=True)
        wide = jnp.pad(weight * (pick_score - mean_score), ((0, 0), (0, LANES - picks)))
        logit_grad_ref[...] = wide.T[:picks, :]


def read_call(core, packed, fetched, gate, grad, last=None):
    tokens, width = gate.shape
    slot_count = packed.shape[1]
    steps = width // 2 // COLS
    own = last is not None
    whole = lambda i, core: (0, 0)

    def by_cols(i, core):
        half = core[0] if own else 1 - core[0]
        return (0, half * steps + i)

    columns = pl.BlockSpec((tokens, COLS), by_cols)
    in_specs = [
        pl.BlockSpec((tokens, slot_count), whole),
        pl.BlockSpec((slot_count, COLS), lambda i, core: (0, i)),
        columns,
        columns,
    ]
    out_specs = [columns, columns]
    out_shape = [jax.ShapeDtypeStruct((tokens, width), jnp.bfloat16)] * 2
    args = [packed, fetched, gate, grad]
    aliases = {}
    if own:
        weight, slot, layer_out, gate_grad, score = last
        picks = weight.shape[1]
        slot = jnp.pad(slot, ((0, 0), (0, LANES - picks)))
        args += [weight, slot, score, layer_out, gate_grad]
        in_specs += [pl.BlockSpec(one.shape, whole) for one in (weight, slot, score)]
        in_specs += [pl.BlockSpec(memory_space=pl.ANY)] * 2
        out_specs.append(pl.BlockSpec((picks, tokens), whole))
        out_shape.append(jax.ShapeDtypeStruct((picks, tokens), jnp.float32))
        aliases = {8: 0, 9: 1}
    else:
        out_specs.append(pl.BlockSpec((tokens, slot_count), whole))
        out_shape.append(jax.ShapeDtypeStruct((tokens, slot_count), jnp.float32))
    return pl.pallas_call(
        functools.partial(read_kernel, own),
        grid_spec=pltpu.PrefetchScalarGridSpec(
            num_scalar_prefetch=1,
            grid=(steps,),
            in_specs=in_specs,
            out_specs=out_specs,
            scratch_shapes=[
                pltpu.VMEM((slot_count, COLS), jnp.bfloat16),
                pltpu.VMEM((tokens, slot_count), jnp.float32),
            ],
        ),
        out_shape=out_shape,
        input_output_aliases=aliases,
        compiler_params=pltpu.CompilerParams(vmem_limit_bytes=VMEM_BYTES),
        cost_estimate=pl.CostEstimate(
            flops=2 * tokens * slot_count * width, bytes_accessed=9 * 2**20, transcendentals=tokens * width // 2
        ),
        name="read_and_scores",
    )(core, *args)


def place_of(core, shifted):
    spot = [(one - core) % RING for one in shifted]
    return (spot[0] * RING + spot[1]) * RING + spot[2]


def shifted_of(core, index):
    return [(one + core) % RING for one in (index // RING**2, index // RING % RING, index % RING)]


def swap(x, axis):
    pairs = []
    for core in range(2):
        for index in range(RING**3):
            shifted = shifted_of(core, index)
            shifted[axis] ^= 1
            pairs.append((core * RING**3 + index, core * RING**3 + place_of(core, shifted)))
    return lax.ppermute(x, ("batch", "table"), pairs)


def swap_cores(x):
    return lax.ppermute(x, "batch", [(0, 1), (1, 0)])


def cube_exchange(x):
    groups = []
    for core in range(2):
        found = {}
        for index in range(RING**3):
            shifted = shifted_of(core, index)
            group = tuple((one + 1) % RING // 2 for one in shifted)
            order = sum(bit * (one // 2) for bit, one in zip(BITS, shifted))
            found.setdefault(group, {})[order] = core * RING**3 + index
        groups += [[members[n] for n in range(CUBE)] for _, members in sorted(found.items())]
    return lax.all_to_all(
        x, ("batch", "table"), split_axis=0, concat_axis=0, axis_index_groups=groups, tiled=True
    )


def after(first, then):
    count = len(first)
    return lax.optimization_barrier((*first, *then))[count:]


def local(
    gate_pre, pick_logits, requests, slot_of_pick, values, first_moment, second_moment, out_grad
):
    capacity, table_size = requests.shape
    slot_count = capacity * table_size
    row_count, width = values.shape
    half_width = width // 2
    core = lax.axis_index("batch")
    shifted = shifted_of(core, lax.axis_index("table"))
    inside = sum(bit * (one % 2) for bit, one in zip(BITS, shifted))
    spot = inside.astype(jnp.int32).reshape(1)
    which = core.astype(jnp.int32).reshape(1)

    mine = lax.dynamic_slice(values, (0, core * half_width), (row_count, half_width))
    parts = [mine[:, chunk * CHUNK : (chunk + 1) * CHUNK] for chunk in range(len(ORDERS))]
    swapped = [swap(part, order[0]) for part, order in zip(parts, ORDERS)]

    lists = jnp.stack([requests, swap_cores(requests)]).reshape(2, capacity, RING, RING, RING)
    for axis in range(2, 5):
        turned = jnp.concatenate(
            [lax.slice_in_dim(lists, RING - 1, RING, axis=axis), lax.slice_in_dim(lists, 0, RING - 1, axis=axis)],
            axis=axis,
        )
        lists = jnp.where(core == 0, lists, turned)
    lists = lists.reshape(2, capacity, 2, 2, 2, 2, 2, 2).transpose(2, 4, 6, 0, 3, 5, 7, 1)
    lists = lists.reshape(2 * CUBE, ROW_BLOCK).astype(jnp.float32)

    gated, gated_theirs = gated_call(which, gate_pre, out_grad)
    gated_other = swap_cores(gated_theirs)
    swapped = after([gated], swapped)
    parts = [jnp.concatenate(pair, axis=0) for pair in zip(parts, swapped)]
    swapped = [swap(part, order[1]) for part, order in zip(parts, ORDERS)]
    slot = (slot_of_pick % table_size) * capacity + slot_of_pick // table_size
    (slot,) = after(parts, [slot])
    packed, weight = pack_call(pick_logits, slot, slot_count)
    packed_other = swap_cores(packed)
    slot_grad = slot_grad_call(which, lists, packed, packed_other, gated, gated_other)
    swapped = after([slot_grad], swapped)
    (slot_grad,) = after(swapped, [slot_grad])
    arrived = cube_exchange(slot_grad)
    parts = [jnp.concatenate(pair, axis=0) for pair in zip(parts, swapped)]
    swapped = [swap(part, order[2]) for part, order in zip(parts, ORDERS)]
    gathered = [half for pair in zip(parts, swapped) for half in pair]
    (arrived,) = after(swapped, [arrived])

    found_other = select_call(1, spot, arrived, gathered)
    fetched_theirs = cube_exchange(found_other)
    (arrived,) = after([found_other], [arrived])
    halves = [partial_call(chunk, spot, arrived, row_count) for chunk in range(len(ORDERS))]
    (arrived,) = after([keep for keep, _ in halves], [arrived])
    found = select_call(0, spot, arrived, gathered)
    received = [swap(send, order[2]) for (_, send), order in zip(halves, ORDERS)]
    received = after([found], received)
    half = CUBE // 4 * row_count
    totals = [keep + other.astype(jnp.float32) for (keep, _), other in zip(halves, received)]
    halves = [(total[:half], total[half:].astype(jnp.bfloat16)) for total in totals]
    received = [swap(send, order[1]) for (_, send), order in zip(halves, ORDERS)]
    (fetched_theirs,) = after([send for _, send in halves], [fetched_theirs])
    (found,) = after([fetched_theirs, *received], [found])
    fetched = cube_exchange(found)
    fetched_other = swap_cores(fetched_theirs)

    half //= 2
    totals = [keep + other.astype(jnp.float32) for (keep, _), other in zip(halves, received)]
    halves = [(total[:half], total[half:].astype(jnp.bfloat16)) for total in totals]
    received = [swap(send, order[0]) for (_, send), order in zip(halves, ORDERS)]
    layer_out, gate_grad, score = read_call(which, packed, fetched_other, gate_pre, out_grad)
    received = after([score], received)
    totals = [keep + other.astype(jnp.float32) for (keep, _), other in zip(halves, received)]
    own = jnp.concatenate(totals, axis=1)
    value_next, first_next, second_next = adam_call(
        which, own, swap_cores(own), values, first_moment, second_moment
    )
    (fetched,) = after([value_next], [fetched])
    layer_out, gate_grad, logit_grad = read_call(
        which, packed, fetched, gate_pre, out_grad, (weight, slot, layer_out, gate_grad, score)
    )
    return (layer_out, gate_grad, logit_grad.T, value_next, first_next, second_next)


def solution(mesh):
    tokens = P(("batch", "table"), None)
    rows = P("table", None)
    return jax.shard_map(
        local,
        mesh=mesh,
        in_specs=(tokens, tokens, tokens, tokens, rows, rows, rows, tokens),
        out_specs=(tokens, tokens, tokens, rows, rows, rows),
        check_vma=False,
    )
```

```python
import functools

import jax
import jax.numpy as jnp
from jax import lax
from jax.experimental import pallas as pl
from jax.experimental.pallas import tpu as pltpu
from jax.sharding import PartitionSpec as P

learn_rate = 0.001
LANES = 128
COLS = 512
RING = 4
CAPACITY = 16
CUBE = 8
BITS = (4, 2, 1)
ORDERS = ((0, 1, 2), (1, 2, 0), (2, 0, 1))
VMEM_BYTES = 60 * 1024 * 1024


CHUNK = 768
ROW_BLOCK = LANES


def chunk_width(chunk, total):
    return min(CHUNK, total - chunk * CHUNK)


def slot_place(owner, shift):
    spot = (owner // RING**2, owner // RING % RING, owner % RING)
    places = []
    for core in range(2):
        shifted = [(one + core) % RING for one in spot]
        cube = sum(bit * (one // 2) for bit, one in zip(BITS, shifted))
        chip = sum(bit * (one % 2) for bit, one in zip(BITS, shifted))
        places.append((cube, chip))
    (cube_0, chip_0), (cube_1, chip_1) = places
    cube = cube_0 + shift * (cube_1 - cube_0)
    chip = chip_0 + shift * (chip_1 - chip_0)
    return cube, chip


def pack_kernel(logit_ref, slot_ref, packed_ref, weight_ref):
    tokens, picks = logit_ref.shape
    slot_count = packed_ref.shape[1]
    logits = logit_ref[...]
    raised = jnp.exp(logits - jnp.max(logits, axis=-1, keepdims=True))
    weight_ref[...] = raised / jnp.sum(raised, axis=-1, keepdims=True)
    rows = 16

    @pl.loop(0, tokens // rows)
    def _(step):
        here = pl.ds(pl.multiple_of(step * rows, rows), rows)
        weight = weight_ref[here, :]
        slot = slot_ref[here, :]
        lane = lax.broadcasted_iota(jnp.int32, (rows, slot_count), 1)
        total = jnp.zeros((rows, slot_count), jnp.float32)
        for k in range(picks):
            total = jnp.where(lane == slot[:, k : k + 1], weight[:, k : k + 1], total)
        packed_ref[here, :] = total.astype(jnp.bfloat16)


def pack_call(logits, slot, slot_count):
    tokens, picks = logits.shape
    return pl.pallas_call(
        pack_kernel,
        out_shape=[
            jax.ShapeDtypeStruct((tokens, slot_count), jnp.bfloat16),
            jax.ShapeDtypeStruct((tokens, picks), jnp.float32),
        ],
        compiler_params=pltpu.CompilerParams(vmem_limit_bytes=VMEM_BYTES),
        cost_estimate=pl.CostEstimate(
            flops=2**25, bytes_accessed=2**20, transcendentals=tokens * picks
        ),
        name="pack_weights",
    )(logits, slot)


def gated_kernel(core_ref, gate_a, grad_a, gate_b, grad_b, mine_ref, theirs_ref):
    for gate_ref, grad_ref, out_ref in ((gate_a, grad_a, mine_ref), (gate_b, grad_b, theirs_ref)):
        gate = gate_ref[...].astype(jnp.float32)
        silu = gate * jax.nn.sigmoid(gate)
        out_ref[...] = (grad_ref[...].astype(jnp.float32) * silu).astype(jnp.bfloat16)


def gated_call(core, gate, grad):
    tokens, width = gate.shape
    steps = width // 2 // COLS
    mine = pl.BlockSpec((tokens, COLS), lambda i, core: (0, core[0] * steps + i))
    theirs = pl.BlockSpec((tokens, COLS), lambda i, core: (0, (1 - core[0]) * steps + i))
    half = pl.BlockSpec((tokens, COLS), lambda i, core: (0, i))
    return pl.pallas_call(
        gated_kernel,
        grid_spec=pltpu.PrefetchScalarGridSpec(
            num_scalar_prefetch=1,
            grid=(steps,),
            in_specs=[mine, mine, theirs, theirs],
            out_specs=[half, half],
        ),
        out_shape=[jax.ShapeDtypeStruct((tokens, width // 2), jnp.bfloat16)] * 2,
        compiler_params=pltpu.CompilerParams(vmem_limit_bytes=VMEM_BYTES),
        cost_estimate=pl.CostEstimate(
            flops=4 * tokens * width, bytes_accessed=6 * tokens * width, transcendentals=tokens * width
        ),
        name="gated_halves",
    )(core, gate, grad, gate, grad)


def slot_grad_kernel(
    core_ref, packed_ref, packed_other_ref, gated_ref, gated_other_ref, slot_grad_ref, turned_ref
):
    slot_count = packed_ref.shape[1]
    groups = ((packed_ref, gated_ref), (packed_other_ref, gated_other_ref))

    @pl.when(pl.program_id(0) == 0)
    def _():
        for group, (weights, _) in enumerate(groups):
            turned_ref[group] = weights[...].T

    for group, (_, gated) in enumerate(groups):
        found = jnp.dot(
            turned_ref[group], gated[...], preferred_element_type=jnp.float32
        ).astype(jnp.bfloat16)
        for owner in range(slot_count // CAPACITY):
            cube, chip = slot_place(owner, core_ref[0])
            start = (cube * 2 + group) * ROW_BLOCK + chip * CAPACITY
            slot_grad_ref[pl.ds(pl.multiple_of(start, CAPACITY), CAPACITY), :] = found[
                owner * CAPACITY : (owner + 1) * CAPACITY, :
            ]


def slot_grad_call(core, packed, packed_other, gated, gated_other):
    tokens, half = gated.shape
    slot_count = packed.shape[1]
    whole = lambda i: (0, 0)
    by_cols = lambda i: (0, i)
    weights = pl.BlockSpec((tokens, slot_count), whole)
    columns = pl.BlockSpec((tokens, COLS), by_cols)
    return pl.pallas_call(
        slot_grad_kernel,
        grid=(half // COLS,),
        in_specs=[pl.BlockSpec(memory_space=pltpu.SMEM), weights, weights, columns, columns],
        out_specs=pl.BlockSpec((2 * slot_count, COLS), by_cols),
        out_shape=jax.ShapeDtypeStruct((2 * slot_count, half), jnp.bfloat16),
        scratch_shapes=[pltpu.VMEM((2, slot_count, tokens), jnp.bfloat16)],
        compiler_params=pltpu.CompilerParams(vmem_limit_bytes=VMEM_BYTES),
        cost_estimate=pl.CostEstimate(
            flops=4 * tokens * slot_count * half, bytes_accessed=14 * 2**20, transcendentals=0
        ),
        name="slot_gradients",
    )(core, packed, packed_other, gated, gated_other)


def spread_kernel(list_ref, spread_ref):
    ones = jnp.ones((LANES, LANES), jnp.bfloat16)
    row = lax.broadcasted_iota(jnp.int32, (LANES, LANES), 0)
    lane = lax.broadcasted_iota(jnp.int32, (LANES, LANES), 1)
    for block in range(list_ref.shape[0]):
        diagonal = jnp.where(row == lane, list_ref[block : block + 1, :], 0.0)
        spread_ref[block * LANES : (block + 1) * LANES, :] = jnp.dot(
            diagonal.astype(jnp.bfloat16), ones, preferred_element_type=jnp.float32
        ).astype(jnp.bfloat16)


def spread_call(lists):
    return pl.pallas_call(
        spread_kernel,
        out_shape=jax.ShapeDtypeStruct((lists.size, LANES), jnp.bfloat16),
        name="spread_lists",
    )(lists)


def relative(order, position):
    return sum(BITS[axis] for bit, axis in enumerate(order) if position >> bit & 1)


def asked_at(owner, peer, group):
    start = (peer * 2 + group) * ROW_BLOCK + owner * CAPACITY
    return pl.ds(pl.multiple_of(start, CAPACITY), CAPACITY)


def asked_rows(ref, owner, groups):
    return jnp.concatenate(
        [ref[asked_at(owner, peer, group), :] for peer in range(CUBE) for group in groups], axis=0
    )


def chosen_rows(id_ref, owner, groups):
    ids = asked_rows(id_ref, owner, groups)
    lane = lax.broadcasted_iota(jnp.int32, ids.shape, 1)
    return (ids.astype(jnp.float32) == lane.astype(jnp.float32)).astype(jnp.bfloat16)


def select_kernel(group, spot_ref, id_ref, *refs):
    out_ref = refs[-1]
    for chunk, order in enumerate(ORDERS):
        near, far = refs[2 * chunk], refs[2 * chunk + 1]
        rows = near.shape[0] * 2 // CUBE

        @pl.when(pl.program_id(0) == chunk)
        def _(order=order, near=near, far=far, rows=rows):
            for position in range(CUBE):
                source = near if position < CUBE // 2 else far
                start = position % (CUBE // 2) * rows
                owner = spot_ref[0] ^ relative(order, position)
                found = jnp.dot(
                    chosen_rows(id_ref, owner, (group,)),
                    source[start : start + rows, :],
                    preferred_element_type=jnp.float32,
                ).astype(jnp.bfloat16)
                for peer in range(CUBE):
                    at = pl.ds(
                        pl.multiple_of(peer * ROW_BLOCK + owner * CAPACITY, CAPACITY), CAPACITY
                    )
                    out_ref[at, : found.shape[1]] = found[peer * CAPACITY : (peer + 1) * CAPACITY, :]


def select_call(group, spot, ids, parts, half_width):
    rows, wide = ids.shape[0], half_width + LANES
    whole = lambda i: (0, 0)
    return pl.pallas_call(
        functools.partial(select_kernel, group),
        grid=(len(ORDERS),),
        in_specs=[
            pl.BlockSpec(memory_space=pltpu.SMEM),
            pl.BlockSpec(ids.shape, whole),
        ]
        + [pl.BlockSpec(part.shape, whole) for part in parts],
        out_specs=pl.BlockSpec((rows // 2, CHUNK), lambda i: (0, i)),
        out_shape=jax.ShapeDtypeStruct((rows // 2, wide - LANES), jnp.bfloat16),
        compiler_params=pltpu.CompilerParams(vmem_limit_bytes=VMEM_BYTES),
        cost_estimate=pl.CostEstimate(
            flops=rows * LANES * wide, bytes_accessed=3 * rows * wide, transcendentals=0
        ),
        name="select_rows",
    )(spot, ids, *parts)


def partial_kernel(chunk, spot_ref, id_ref, arrived_ref, keep_ref, send_ref):
    rows = keep_ref.shape[0] * 2 // CUBE
    cols = keep_ref.shape[1]
    for position in range(CUBE):
        owner = spot_ref[0] ^ relative(ORDERS[chunk], position)
        chosen = chosen_rows(id_ref, owner, (0, 1))
        by_rows = (((0,), (0,)), ((), ()))
        total = lax.dot_general(
            chosen, asked_rows(arrived_ref, owner, (0, 1))[:, :cols], by_rows,
            preferred_element_type=jnp.float32,
        )
        target = keep_ref if position < CUBE // 2 else send_ref
        start = position % (CUBE // 2) * rows
        target[start : start + rows, :] = total.astype(target.dtype)
        if chunk == len(ORDERS) - 1:
            hits = lax.dot_general(
                chosen, jnp.ones(chosen.shape, jnp.bfloat16), by_rows, preferred_element_type=jnp.float32
            )
            target[start : start + rows, cols - LANES :] = hits.astype(target.dtype)


def partial_call(chunk, spot, ids, arrived, row_count):
    rows, wide = arrived.shape[0], arrived.shape[1] + LANES
    cols = chunk_width(chunk, wide)
    half = CUBE // 2 * row_count
    whole = lambda i: (0, 0)
    return pl.pallas_call(
        functools.partial(partial_kernel, chunk),
        grid=(1,),
        in_specs=[
            pl.BlockSpec(memory_space=pltpu.SMEM),
            pl.BlockSpec(ids.shape, whole),
            pl.BlockSpec((rows, CHUNK), lambda i: (0, chunk)),
        ],
        out_specs=[pl.BlockSpec((half, cols), whole)] * 2,
        out_shape=[
            jax.ShapeDtypeStruct((half, cols), jnp.float32),
            jax.ShapeDtypeStruct((half, cols), jnp.bfloat16),
        ],
        compiler_params=pltpu.CompilerParams(vmem_limit_bytes=VMEM_BYTES),
        cost_estimate=pl.CostEstimate(
            flops=2 * rows * LANES * cols, bytes_accessed=8 * rows * cols, transcendentals=0
        ),
        name="partial_sums",
    )(spot, ids, arrived)


def adam_kernel(
    core_ref, hits_ref, own_ref, other_ref, value_ref, first_ref, second_ref,
    value_out, first_out, second_out,
):
    touched = hits_ref[...][:, :1] > 0.0
    own = pl.program_id(0) < pl.num_programs(0) // 2
    row_grad = jnp.where(own, own_ref[...], other_ref[...])
    first = first_ref[...]
    second = second_ref[...]
    value = value_ref[...].astype(jnp.float32)
    first_new = 0.9 * first + 0.1 * row_grad
    second_new = 0.95 * second + 0.05 * row_grad * row_grad
    value_new = value - learn_rate * first_new / (jnp.sqrt(second_new) + 1e-08)
    value_out[...] = jnp.where(touched, value_new, value).astype(jnp.bfloat16)
    first_out[...] = jnp.where(touched, first_new, first)
    second_out[...] = jnp.where(touched, second_new, second)


def adam_call(core, own, other, values, first, second):
    rows, width = values.shape
    steps = width // 2 // COLS
    columns = pl.BlockSpec(
        (rows, COLS),
        lambda i, core: (0, lax.rem(core[0] + i // steps, 2) * steps + lax.rem(i, steps)),
    )
    return pl.pallas_call(
        adam_kernel,
        grid_spec=pltpu.PrefetchScalarGridSpec(
            num_scalar_prefetch=1,
            grid=(2 * steps,),
            in_specs=[
                pl.BlockSpec((rows, LANES), lambda i, core: (0, width // 2 // LANES)),
                pl.BlockSpec((rows, COLS), lambda i, core: (0, jnp.minimum(i, steps - 1))),
                pl.BlockSpec((rows, COLS), lambda i, core: (0, jnp.maximum(i - steps, 0))),
                columns, columns, columns,
            ],
            out_specs=[columns] * 3,
        ),
        out_shape=[
            jax.ShapeDtypeStruct(values.shape, values.dtype),
            jax.ShapeDtypeStruct(first.shape, first.dtype),
            jax.ShapeDtypeStruct(second.shape, second.dtype),
        ],
        compiler_params=pltpu.CompilerParams(vmem_limit_bytes=VMEM_BYTES),
        cost_estimate=pl.CostEstimate(
            flops=10 * rows * width, bytes_accessed=28 * rows * width, transcendentals=rows * width
        ),
        name="adam_rows",
    )(core, own, own, other, values, first, second)


def read_kernel(own, core_ref, packed_ref, fetched_ref, gate_ref, grad_ref, *refs):
    if own:
        weight_ref, slot_ref, before_ref, _, _, out_ref, gate_grad_ref, logit_grad_ref = refs[:8]
    else:
        out_ref, gate_grad_ref, score_out_ref = refs[:3]
    ordered_ref, score_ref = refs[-2:]
    step = pl.program_id(0)
    shift = core_ref[0] if own else 1 - core_ref[0]
    for owner in range(ordered_ref.shape[0] // CAPACITY):
        cube, chip = slot_place(owner, shift)
        at = pl.ds(pl.multiple_of(cube * ROW_BLOCK + chip * CAPACITY, CAPACITY), CAPACITY)
        ordered_ref[owner * CAPACITY : (owner + 1) * CAPACITY, :] = fetched_ref[at, :]
    fetched = ordered_ref[...]
    memory = jnp.dot(packed_ref[...], fetched, preferred_element_type=jnp.float32)
    gate = gate_ref[...].astype(jnp.float32)
    sig = jax.nn.sigmoid(gate)
    silu = gate * sig
    grad = grad_ref[...].astype(jnp.float32)
    out_ref[...] = (silu * memory).astype(jnp.bfloat16)
    gated = (grad * silu).astype(jnp.bfloat16)
    gate_grad_ref[...] = (grad * memory * sig * (1.0 + gate * (1.0 - sig))).astype(jnp.bfloat16)
    score = lax.dot_general(
        gated, fetched, (((1,), (1,)), ((), ())), preferred_element_type=jnp.float32
    )

    @pl.when(step == 0)
    def _():
        score_ref[...] = score + before_ref[...] if own else score

    @pl.when(step > 0)
    def _():
        score_ref[...] += score

    @pl.when(step == pl.num_programs(0) - 1)
    def _():
        if not own:
            score_out_ref[...] = score_ref[...]
            return
        picks = weight_ref.shape[1]
        slot = slot_ref[...]
        low = lax.rem(slot, LANES)
        high = slot // LANES
        wide = jnp.zeros(slot.shape, jnp.float32)
        for part in range(score_ref.shape[1] // LANES):
            here = score_ref[:, part * LANES : (part + 1) * LANES]
            wide = jnp.where(high == part, jnp.take_along_axis(here, low, axis=1), wide)
        pick_score = wide[:, :picks]
        weight = weight_ref[...]
        mean_score = jnp.sum(weight * pick_score, axis=-1, keepdims=True)
        wide = jnp.pad(weight * (pick_score - mean_score), ((0, 0), (0, LANES - picks)))
        logit_grad_ref[...] = wide.T[:picks, :]


def read_call(core, packed, fetched, gate, grad, last=None):
    tokens, width = gate.shape
    slot_count = packed.shape[1]
    steps = width // 2 // COLS
    own = last is not None
    whole = lambda i, core: (0, 0)

    def by_cols(i, core):
        half = core[0] if own else 1 - core[0]
        return (0, half * steps + i)

    columns = pl.BlockSpec((tokens, COLS), by_cols)
    in_specs = [
        pl.BlockSpec((tokens, slot_count), whole),
        pl.BlockSpec((slot_count, COLS), lambda i, core: (0, i)),
        columns,
        columns,
    ]
    out_specs = [columns, columns]
    out_shape = [jax.ShapeDtypeStruct((tokens, width), jnp.bfloat16)] * 2
    args = [packed, fetched, gate, grad]
    aliases = {}
    if own:
        weight, slot, layer_out, gate_grad, score = last
        picks = weight.shape[1]
        slot = jnp.pad(slot, ((0, 0), (0, LANES - picks)))
        args += [weight, slot, score, layer_out, gate_grad]
        in_specs += [pl.BlockSpec(one.shape, whole) for one in (weight, slot, score)]
        in_specs += [pl.BlockSpec(memory_space=pl.ANY)] * 2
        out_specs.append(pl.BlockSpec((picks, tokens), whole))
        out_shape.append(jax.ShapeDtypeStruct((picks, tokens), jnp.float32))
        aliases = {8: 0, 9: 1}
    else:
        out_specs.append(pl.BlockSpec((tokens, slot_count), whole))
        out_shape.append(jax.ShapeDtypeStruct((tokens, slot_count), jnp.float32))
    return pl.pallas_call(
        functools.partial(read_kernel, own),
        grid_spec=pltpu.PrefetchScalarGridSpec(
            num_scalar_prefetch=1,
            grid=(steps,),
            in_specs=in_specs,
            out_specs=out_specs,
            scratch_shapes=[
                pltpu.VMEM((slot_count, COLS), jnp.bfloat16),
                pltpu.VMEM((tokens, slot_count), jnp.float32),
            ],
        ),
        out_shape=out_shape,
        input_output_aliases=aliases,
        compiler_params=pltpu.CompilerParams(vmem_limit_bytes=VMEM_BYTES),
        cost_estimate=pl.CostEstimate(
            flops=2 * tokens * slot_count * width, bytes_accessed=9 * 2**20, transcendentals=tokens * width // 2
        ),
        name="read_and_scores",
    )(core, *args)


def place_of(core, shifted):
    spot = [(one - core) % RING for one in shifted]
    return (spot[0] * RING + spot[1]) * RING + spot[2]


def shifted_of(core, index):
    return [(one + core) % RING for one in (index // RING**2, index // RING % RING, index % RING)]


def swap(x, axis, crossing=0):
    pairs = []
    for core in range(2):
        for index in range(RING**3):
            shifted = shifted_of(core, index)
            shifted[axis] = ((shifted[axis] + crossing) ^ 1) - crossing
            pairs.append((core * RING**3 + index, core * RING**3 + place_of(core, shifted)))
    return lax.ppermute(x, ("batch", "table"), pairs)


def swap_cores(x):
    return lax.ppermute(x, "batch", [(0, 1), (1, 0)])


def cube_exchange(x):
    groups = []
    for core in range(2):
        found = {}
        for index in range(RING**3):
            shifted = shifted_of(core, index)
            group = tuple((one + 1) % RING // 2 for one in shifted)
            order = sum(bit * (one // 2) for bit, one in zip(BITS, shifted))
            found.setdefault(group, {})[order] = core * RING**3 + index
        groups += [[members[n] for n in range(CUBE)] for _, members in sorted(found.items())]
    return lax.all_to_all(
        x, ("batch", "table"), split_axis=0, concat_axis=0, axis_index_groups=groups, tiled=True
    )


def after(first, then):
    count = len(first)
    return lax.optimization_barrier((*first, *then))[count:]


def local(
    gate_pre, pick_logits, requests, slot_of_pick, values, first_moment, second_moment, out_grad
):
    capacity, table_size = requests.shape
    slot_count = capacity * table_size
    row_count, width = values.shape
    half_width = width // 2
    core = lax.axis_index("batch")
    shifted = shifted_of(core, lax.axis_index("table"))
    inside = sum(bit * (one % 2) for bit, one in zip(BITS, shifted))
    spot = inside.astype(jnp.int32).reshape(1)
    which = core.astype(jnp.int32).reshape(1)

    mine = lax.dynamic_slice(values, (0, core * half_width), (row_count, half_width))
    parts = [mine[:, chunk * CHUNK : (chunk + 1) * CHUNK] for chunk in range(len(ORDERS))]
    swapped = [swap(part, order[0]) for part, order in zip(parts, ORDERS)]

    lists = jnp.stack([requests, swap_cores(requests)]).reshape(2, capacity, RING, RING, RING)
    for axis in range(2, 5):
        turned = jnp.concatenate(
            [lax.slice_in_dim(lists, RING - 1, RING, axis=axis), lax.slice_in_dim(lists, 0, RING - 1, axis=axis)],
            axis=axis,
        )
        lists = jnp.where(core == 0, lists, turned)
    lists = lists.reshape(2, capacity, 2, 2, 2, 2, 2, 2).transpose(2, 4, 6, 0, 3, 5, 7, 1)
    lists = lists.reshape(2 * CUBE, ROW_BLOCK).astype(jnp.float32)

    lists = lists[None]
    (which_late,) = after([lists], [which])
    crossed = swap(lists, 0, 1)
    gated, gated_theirs = gated_call(which_late, gate_pre, out_grad)
    gated_other = swap_cores(gated_theirs)
    swapped = after([gated], swapped)
    (crossed,) = after([gated], [crossed])
    lists = jnp.concatenate([lists, crossed], axis=0)
    crossed = swap(lists, 1, 1)
    parts = [jnp.concatenate(pair, axis=0) for pair in zip(parts, swapped)]
    swapped = [swap(part, order[1]) for part, order in zip(parts, ORDERS)]
    slot = (slot_of_pick % table_size) * capacity + slot_of_pick // table_size
    (slot,) = after(parts, [slot])
    packed, weight = pack_call(pick_logits, slot, slot_count)
    packed_other = swap_cores(packed)
    (crossed,) = after([packed], [crossed])
    lists = jnp.concatenate([lists, crossed], axis=0)
    crossed = swap(lists, 2, 1)
    slot_grad = slot_grad_call(which, packed, packed_other, gated, gated_other)
    swapped = after([slot_grad], swapped)
    (crossed,) = after([slot_grad], [crossed])
    (slot_grad,) = after([crossed, *swapped], [slot_grad])
    arrived = cube_exchange(slot_grad)
    parts = [jnp.concatenate(pair, axis=0) for pair in zip(parts, swapped)]
    swapped = [swap(part, order[2]) for part, order in zip(parts, ORDERS)]
    gathered = [half for pair in zip(parts, swapped) for half in pair]

    lists = jnp.concatenate([lists, crossed], axis=0)
    own_cube = sum(bit * (one // 2) for bit, one in zip(BITS, shifted))
    lists = lists.reshape(CUBE, CUBE, 2, ROW_BLOCK)
    lists = lax.dynamic_slice(lists, (0, own_cube, 0, 0), (CUBE, 1, 2, ROW_BLOCK))
    lists = lists.reshape(2, 2, 2, 2, ROW_BLOCK).transpose(2, 1, 0, 3, 4)
    for axis in range(3):
        lists = jnp.where(shifted[axis] // 2 == 0, lists, jnp.flip(lists, axis))
    ids = spread_call(lists.reshape(2 * CUBE, ROW_BLOCK))
    found_other = select_call(1, spot, ids, gathered, half_width)
    (arrived,) = after([found_other], [arrived])
    (found_other,) = after([arrived], [found_other])
    fetched_theirs = cube_exchange(found_other)

    halves = [partial_call(chunk, spot, ids, arrived, row_count) for chunk in range(len(ORDERS))]
    (ids,) = after([keep for keep, _ in halves], [ids])
    found = select_call(0, spot, ids, gathered, half_width)
    received = [swap(send, order[2]) for (_, send), order in zip(halves, ORDERS)]
    received = after([found], received)
    half = CUBE // 4 * row_count
    totals = [keep + other.astype(jnp.float32) for (keep, _), other in zip(halves, received)]
    halves = [(total[:half], total[half:].astype(jnp.bfloat16)) for total in totals]
    received = [swap(send, order[1]) for (_, send), order in zip(halves, ORDERS)]
    (fetched_theirs,) = after([send for _, send in halves], [fetched_theirs])
    (found,) = after([fetched_theirs, *received], [found])
    fetched = cube_exchange(found)
    fetched_other = swap_cores(fetched_theirs)

    half //= 2
    totals = [keep + other.astype(jnp.float32) for (keep, _), other in zip(halves, received)]
    halves = [(total[:half], total[half:].astype(jnp.bfloat16)) for total in totals]
    received = [swap(send, order[0]) for (_, send), order in zip(halves, ORDERS)]
    layer_out, gate_grad, score = read_call(which, packed, fetched_other, gate_pre, out_grad)
    received = after([score], received)
    totals = [keep + other.astype(jnp.float32) for (keep, _), other in zip(halves, received)]
    own = jnp.concatenate(totals, axis=1)
    value_next, first_next, second_next = adam_call(
        which, own, swap_cores(own), values, first_moment, second_moment
    )
    (fetched,) = after([value_next], [fetched])
    layer_out, gate_grad, logit_grad = read_call(
        which, packed, fetched, gate_pre, out_grad, (weight, slot, layer_out, gate_grad, score)
    )
    return (layer_out, gate_grad, logit_grad.T, value_next, first_next, second_next)


def solution(mesh):
    tokens = P(("batch", "table"), None)
    rows = P("table", None)
    return jax.shard_map(
        local,
        mesh=mesh,
        in_specs=(tokens, tokens, tokens, tokens, rows, rows, rows, tokens),
        out_specs=(tokens, tokens, tokens, rows, rows, rows),
        check_vma=False,
    )
```

```python
import functools

import jax
import jax.numpy as jnp
from jax import lax
from jax.experimental import pallas as pl
from jax.experimental.pallas import tpu as pltpu
from jax.sharding import PartitionSpec as P

learn_rate = 0.001
LANES = 128
COLS = 512
RING = 4
CAPACITY = 16
CUBE = 8
BITS = (4, 2, 1)
ORDERS = ((0, 1, 2), (1, 2, 0), (2, 0, 1))
VMEM_BYTES = 60 * 1024 * 1024


CHUNK = 768
ROW_BLOCK = LANES


def chunk_width(chunk, total):
    return min(CHUNK, total - chunk * CHUNK)


def slot_place(owner, shift):
    spot = (owner // RING**2, owner // RING % RING, owner % RING)
    places = []
    for core in range(2):
        shifted = [(one + core) % RING for one in spot]
        cube = sum(bit * (one // 2) for bit, one in zip(BITS, shifted))
        chip = sum(bit * (one % 2) for bit, one in zip(BITS, shifted))
        places.append((cube, chip))
    (cube_0, chip_0), (cube_1, chip_1) = places
    cube = cube_0 + shift * (cube_1 - cube_0)
    chip = chip_0 + shift * (chip_1 - chip_0)
    return cube, chip


def pack_kernel(logit_ref, slot_ref, packed_ref, weight_ref):
    tokens, picks = logit_ref.shape
    slot_count = packed_ref.shape[1]
    logits = logit_ref[...]
    raised = jnp.exp(logits - jnp.max(logits, axis=-1, keepdims=True))
    weight_ref[...] = raised / jnp.sum(raised, axis=-1, keepdims=True)
    rows = 16

    @pl.loop(0, tokens // rows)
    def _(step):
        here = pl.ds(pl.multiple_of(step * rows, rows), rows)
        weight = weight_ref[here, :]
        slot = slot_ref[here, :]
        lane = lax.broadcasted_iota(jnp.int32, (rows, slot_count), 1)
        total = jnp.zeros((rows, slot_count), jnp.float32)
        for k in range(picks):
            total = jnp.where(lane == slot[:, k : k + 1], weight[:, k : k + 1], total)
        packed_ref[here, :] = total.astype(jnp.bfloat16)


def pack_call(logits, slot, slot_count):
    tokens, picks = logits.shape
    return pl.pallas_call(
        pack_kernel,
        out_shape=[
            jax.ShapeDtypeStruct((tokens, slot_count), jnp.bfloat16),
            jax.ShapeDtypeStruct((tokens, picks), jnp.float32),
        ],
        compiler_params=pltpu.CompilerParams(vmem_limit_bytes=VMEM_BYTES),
        cost_estimate=pl.CostEstimate(
            flops=2**25, bytes_accessed=2**20, transcendentals=tokens * picks
        ),
        name="pack_weights",
    )(logits, slot)


def gated_kernel(core_ref, gate_a, grad_a, gate_b, grad_b, mine_ref, theirs_ref):
    for gate_ref, grad_ref, out_ref in ((gate_a, grad_a, mine_ref), (gate_b, grad_b, theirs_ref)):
        gate = gate_ref[...].astype(jnp.float32)
        silu = gate * jax.nn.sigmoid(gate)
        out_ref[...] = (grad_ref[...].astype(jnp.float32) * silu).astype(jnp.bfloat16)


def gated_call(core, gate, grad):
    tokens, width = gate.shape
    steps = width // 2 // COLS
    mine = pl.BlockSpec((tokens, COLS), lambda i, core: (0, core[0] * steps + i))
    theirs = pl.BlockSpec((tokens, COLS), lambda i, core: (0, (1 - core[0]) * steps + i))
    half = pl.BlockSpec((tokens, COLS), lambda i, core: (0, i))
    return pl.pallas_call(
        gated_kernel,
        grid_spec=pltpu.PrefetchScalarGridSpec(
            num_scalar_prefetch=1,
            grid=(steps,),
            in_specs=[mine, mine, theirs, theirs],
            out_specs=[half, half],
        ),
        out_shape=[jax.ShapeDtypeStruct((tokens, width // 2), jnp.bfloat16)] * 2,
        compiler_params=pltpu.CompilerParams(vmem_limit_bytes=VMEM_BYTES),
        cost_estimate=pl.CostEstimate(
            flops=4 * tokens * width, bytes_accessed=6 * tokens * width, transcendentals=tokens * width
        ),
        name="gated_halves",
    )(core, gate, grad, gate, grad)


def slot_grad_kernel(
    core_ref, packed_ref, packed_other_ref, gated_ref, gated_other_ref, slot_grad_ref, turned_ref
):
    slot_count = packed_ref.shape[1]
    groups = ((packed_ref, gated_ref), (packed_other_ref, gated_other_ref))

    @pl.when(pl.program_id(0) == 0)
    def _():
        for group, (weights, _) in enumerate(groups):
            turned_ref[group] = weights[...].T

    for group, (_, gated) in enumerate(groups):
        found = jnp.dot(
            turned_ref[group], gated[...], preferred_element_type=jnp.float32
        ).astype(jnp.bfloat16)
        for owner in range(slot_count // CAPACITY):
            cube, chip = slot_place(owner, core_ref[0])
            start = (cube * 2 + group) * ROW_BLOCK + chip * CAPACITY
            slot_grad_ref[pl.ds(pl.multiple_of(start, CAPACITY), CAPACITY), :] = found[
                owner * CAPACITY : (owner + 1) * CAPACITY, :
            ]


def slot_grad_call(core, packed, packed_other, gated, gated_other):
    tokens, half = gated.shape
    slot_count = packed.shape[1]
    whole = lambda i: (0, 0)
    by_cols = lambda i: (0, i)
    weights = pl.BlockSpec((tokens, slot_count), whole)
    columns = pl.BlockSpec((tokens, COLS), by_cols)
    return pl.pallas_call(
        slot_grad_kernel,
        grid=(half // COLS,),
        in_specs=[pl.BlockSpec(memory_space=pltpu.SMEM), weights, weights, columns, columns],
        out_specs=pl.BlockSpec((2 * slot_count, COLS), by_cols),
        out_shape=jax.ShapeDtypeStruct((2 * slot_count, half), jnp.bfloat16),
        scratch_shapes=[pltpu.VMEM((2, slot_count, tokens), jnp.bfloat16)],
        compiler_params=pltpu.CompilerParams(vmem_limit_bytes=VMEM_BYTES),
        cost_estimate=pl.CostEstimate(
            flops=4 * tokens * slot_count * half, bytes_accessed=14 * 2**20, transcendentals=0
        ),
        name="slot_gradients",
    )(core, packed, packed_other, gated, gated_other)


def spread_kernel(list_ref, spread_ref):
    ones = jnp.ones((LANES, LANES), jnp.bfloat16)
    row = lax.broadcasted_iota(jnp.int32, (LANES, LANES), 0)
    lane = lax.broadcasted_iota(jnp.int32, (LANES, LANES), 1)
    for block in range(list_ref.shape[0]):
        diagonal = jnp.where(row == lane, list_ref[block : block + 1, :], 0.0)
        spread_ref[block * LANES : (block + 1) * LANES, :] = jnp.dot(
            diagonal.astype(jnp.bfloat16), ones, preferred_element_type=jnp.float32
        ).astype(jnp.bfloat16)


def spread_call(lists):
    return pl.pallas_call(
        spread_kernel,
        out_shape=jax.ShapeDtypeStruct((lists.size, LANES), jnp.bfloat16),
        name="spread_lists",
    )(lists)


def relative(order, position):
    return sum(BITS[axis] for bit, axis in enumerate(order) if position >> bit & 1)


def asked_at(owner, peer, group):
    start = (peer * 2 + group) * ROW_BLOCK + owner * CAPACITY
    return pl.ds(pl.multiple_of(start, CAPACITY), CAPACITY)


def asked_rows(ref, owner, groups):
    return jnp.concatenate(
        [ref[asked_at(owner, peer, group), :] for peer in range(CUBE) for group in groups], axis=0
    )


def chosen_rows(id_ref, owner, groups):
    ids = asked_rows(id_ref, owner, groups)
    lane = lax.broadcasted_iota(jnp.int32, ids.shape, 1)
    return (ids.astype(jnp.float32) == lane.astype(jnp.float32)).astype(jnp.bfloat16)


def select_kernel(group, spot_ref, id_ref, *refs):
    out_ref = refs[-1]
    for chunk, order in enumerate(ORDERS):
        near, far = refs[2 * chunk], refs[2 * chunk + 1]
        rows = near.shape[0] * 2 // CUBE

        @pl.when(pl.program_id(0) == chunk)
        def _(order=order, near=near, far=far, rows=rows):
            for position in range(CUBE):
                source = near if position < CUBE // 2 else far
                start = position % (CUBE // 2) * rows
                owner = spot_ref[0] ^ relative(order, position)
                found = jnp.dot(
                    chosen_rows(id_ref, owner, (group,)),
                    source[start : start + rows, :],
                    preferred_element_type=jnp.float32,
                ).astype(jnp.bfloat16)
                for peer in range(CUBE):
                    at = pl.ds(
                        pl.multiple_of(peer * ROW_BLOCK + owner * CAPACITY, CAPACITY), CAPACITY
                    )
                    out_ref[at, : found.shape[1]] = found[peer * CAPACITY : (peer + 1) * CAPACITY, :]


def select_call(group, spot, ids, parts, half_width):
    rows, wide = ids.shape[0], half_width + LANES
    whole = lambda i: (0, 0)
    return pl.pallas_call(
        functools.partial(select_kernel, group),
        grid=(len(ORDERS),),
        in_specs=[
            pl.BlockSpec(memory_space=pltpu.SMEM),
            pl.BlockSpec(ids.shape, whole),
        ]
        + [pl.BlockSpec(part.shape, whole) for part in parts],
        out_specs=pl.BlockSpec((rows // 2, CHUNK), lambda i: (0, i)),
        out_shape=jax.ShapeDtypeStruct((rows // 2, wide - LANES), jnp.bfloat16),
        compiler_params=pltpu.CompilerParams(vmem_limit_bytes=VMEM_BYTES),
        cost_estimate=pl.CostEstimate(
            flops=rows * LANES * wide, bytes_accessed=3 * rows * wide, transcendentals=0
        ),
        name="select_rows",
    )(spot, ids, *parts)


def partial_kernel(chunk, spot_ref, id_ref, arrived_ref, keep_ref, send_ref):
    rows = keep_ref.shape[0] * 2 // CUBE
    cols = keep_ref.shape[1]
    for position in range(CUBE):
        owner = spot_ref[0] ^ relative(ORDERS[chunk], position)
        chosen = chosen_rows(id_ref, owner, (0, 1))
        by_rows = (((0,), (0,)), ((), ()))
        total = lax.dot_general(
            chosen, asked_rows(arrived_ref, owner, (0, 1))[:, :cols], by_rows,
            preferred_element_type=jnp.float32,
        )
        target = keep_ref if position < CUBE // 2 else send_ref
        start = position % (CUBE // 2) * rows
        target[start : start + rows, :] = total.astype(target.dtype)
        if chunk == len(ORDERS) - 1:
            hits = lax.dot_general(
                chosen, jnp.ones(chosen.shape, jnp.bfloat16), by_rows, preferred_element_type=jnp.float32
            )
            target[start : start + rows, cols - LANES :] = hits.astype(target.dtype)


def partial_call(chunk, spot, ids, arrived, row_count):
    rows, wide = arrived.shape[0], arrived.shape[1] + LANES
    cols = chunk_width(chunk, wide)
    half = CUBE // 2 * row_count
    whole = lambda i: (0, 0)
    return pl.pallas_call(
        functools.partial(partial_kernel, chunk),
        grid=(1,),
        in_specs=[
            pl.BlockSpec(memory_space=pltpu.SMEM),
            pl.BlockSpec(ids.shape, whole),
            pl.BlockSpec((rows, CHUNK), lambda i: (0, chunk)),
        ],
        out_specs=[pl.BlockSpec((half, cols), whole)] * 2,
        out_shape=[
            jax.ShapeDtypeStruct((half, cols), jnp.float32),
            jax.ShapeDtypeStruct((half, cols), jnp.bfloat16),
        ],
        compiler_params=pltpu.CompilerParams(vmem_limit_bytes=VMEM_BYTES),
        cost_estimate=pl.CostEstimate(
            flops=2 * rows * LANES * cols, bytes_accessed=8 * rows * cols, transcendentals=0
        ),
        name="partial_sums",
    )(spot, ids, arrived)


def adam_kernel(
    core_ref, hits_ref, own_ref, other_ref, value_ref, first_ref, second_ref,
    value_out, first_out, second_out,
):
    touched = hits_ref[...][:, :1] > 0.0
    own = pl.program_id(0) < pl.num_programs(0) // 2
    row_grad = jnp.where(own, own_ref[...], other_ref[...])
    first = first_ref[...]
    second = second_ref[...]
    value = value_ref[...].astype(jnp.float32)
    first_new = 0.9 * first + 0.1 * row_grad
    second_new = 0.95 * second + 0.05 * row_grad * row_grad
    value_new = value - learn_rate * first_new / (jnp.sqrt(second_new) + 1e-08)
    value_out[...] = jnp.where(touched, value_new, value).astype(jnp.bfloat16)
    first_out[...] = jnp.where(touched, first_new, first)
    second_out[...] = jnp.where(touched, second_new, second)


def adam_call(core, own, other, values, first, second):
    rows, width = values.shape
    steps = width // 2 // COLS
    columns = pl.BlockSpec(
        (rows, COLS),
        lambda i, core: (0, lax.rem(core[0] + i // steps, 2) * steps + lax.rem(i, steps)),
    )
    return pl.pallas_call(
        adam_kernel,
        grid_spec=pltpu.PrefetchScalarGridSpec(
            num_scalar_prefetch=1,
            grid=(2 * steps,),
            in_specs=[
                pl.BlockSpec((rows, LANES), lambda i, core: (0, width // 2 // LANES)),
                pl.BlockSpec((rows, COLS), lambda i, core: (0, jnp.minimum(i, steps - 1))),
                pl.BlockSpec((rows, COLS), lambda i, core: (0, jnp.maximum(i - steps, 0))),
                columns, columns, columns,
            ],
            out_specs=[columns] * 3,
        ),
        out_shape=[
            jax.ShapeDtypeStruct(values.shape, values.dtype),
            jax.ShapeDtypeStruct(first.shape, first.dtype),
            jax.ShapeDtypeStruct(second.shape, second.dtype),
        ],
        compiler_params=pltpu.CompilerParams(vmem_limit_bytes=VMEM_BYTES),
        cost_estimate=pl.CostEstimate(
            flops=10 * rows * width, bytes_accessed=28 * rows * width, transcendentals=rows * width
        ),
        name="adam_rows",
    )(core, own, own, other, values, first, second)


def read_kernel(own, core_ref, packed_ref, fetched_ref, gate_ref, grad_ref, *refs):
    if own:
        weight_ref, slot_ref, before_ref, _, _, out_ref, gate_grad_ref, logit_grad_ref = refs[:8]
    else:
        out_ref, gate_grad_ref, score_out_ref = refs[:3]
    ordered_ref, score_ref = refs[-2:]
    step = pl.program_id(0)
    shift = core_ref[0] if own else 1 - core_ref[0]
    for owner in range(ordered_ref.shape[0] // CAPACITY):
        cube, chip = slot_place(owner, shift)
        at = pl.ds(pl.multiple_of(cube * ROW_BLOCK + chip * CAPACITY, CAPACITY), CAPACITY)
        ordered_ref[owner * CAPACITY : (owner + 1) * CAPACITY, :] = fetched_ref[at, :]
    fetched = ordered_ref[...]
    memory = jnp.dot(packed_ref[...], fetched, preferred_element_type=jnp.float32)
    gate = gate_ref[...].astype(jnp.float32)
    sig = jax.nn.sigmoid(gate)
    silu = gate * sig
    grad = grad_ref[...].astype(jnp.float32)
    out_ref[...] = (silu * memory).astype(jnp.bfloat16)
    gated = (grad * silu).astype(jnp.bfloat16)
    gate_grad_ref[...] = (grad * memory * sig * (1.0 + gate * (1.0 - sig))).astype(jnp.bfloat16)
    score = lax.dot_general(
        gated, fetched, (((1,), (1,)), ((), ())), preferred_element_type=jnp.float32
    )

    @pl.when(step == 0)
    def _():
        score_ref[...] = score + before_ref[...] if own else score

    @pl.when(step > 0)
    def _():
        score_ref[...] += score

    @pl.when(step == pl.num_programs(0) - 1)
    def _():
        if not own:
            score_out_ref[...] = score_ref[...]
            return
        picks = weight_ref.shape[1]
        slot = slot_ref[...]
        low = lax.rem(slot, LANES)
        high = slot // LANES
        wide = jnp.zeros(slot.shape, jnp.float32)
        for part in range(score_ref.shape[1] // LANES):
            here = score_ref[:, part * LANES : (part + 1) * LANES]
            wide = jnp.where(high == part, jnp.take_along_axis(here, low, axis=1), wide)
        pick_score = wide[:, :picks]
        weight = weight_ref[...]
        mean_score = jnp.sum(weight * pick_score, axis=-1, keepdims=True)
        wide = jnp.pad(weight * (pick_score - mean_score), ((0, 0), (0, LANES - picks)))
        logit_grad_ref[...] = wide.T[:picks, :]


def read_call(core, packed, fetched, gate, grad, last=None):
    tokens, width = gate.shape
    slot_count = packed.shape[1]
    steps = width // 2 // COLS
    own = last is not None
    whole = lambda i, core: (0, 0)

    def by_cols(i, core):
        half = core[0] if own else 1 - core[0]
        return (0, half * steps + i)

    columns = pl.BlockSpec((tokens, COLS), by_cols)
    in_specs = [
        pl.BlockSpec((tokens, slot_count), whole),
        pl.BlockSpec((slot_count, COLS), lambda i, core: (0, i)),
        columns,
        columns,
    ]
    out_specs = [columns, columns]
    out_shape = [jax.ShapeDtypeStruct((tokens, width), jnp.bfloat16)] * 2
    args = [packed, fetched, gate, grad]
    aliases = {}
    if own:
        weight, slot, layer_out, gate_grad, score = last
        picks = weight.shape[1]
        slot = jnp.pad(slot, ((0, 0), (0, LANES - picks)))
        args += [weight, slot, score, layer_out, gate_grad]
        in_specs += [pl.BlockSpec(one.shape, whole) for one in (weight, slot, score)]
        in_specs += [pl.BlockSpec(memory_space=pl.ANY)] * 2
        out_specs.append(pl.BlockSpec((picks, tokens), whole))
        out_shape.append(jax.ShapeDtypeStruct((picks, tokens), jnp.float32))
        aliases = {8: 0, 9: 1}
    else:
        out_specs.append(pl.BlockSpec((tokens, slot_count), whole))
        out_shape.append(jax.ShapeDtypeStruct((tokens, slot_count), jnp.float32))
    return pl.pallas_call(
        functools.partial(read_kernel, own),
        grid_spec=pltpu.PrefetchScalarGridSpec(
            num_scalar_prefetch=1,
            grid=(steps,),
            in_specs=in_specs,
            out_specs=out_specs,
            scratch_shapes=[
                pltpu.VMEM((slot_count, COLS), jnp.bfloat16),
                pltpu.VMEM((tokens, slot_count), jnp.float32),
            ],
        ),
        out_shape=out_shape,
        input_output_aliases=aliases,
        compiler_params=pltpu.CompilerParams(vmem_limit_bytes=VMEM_BYTES),
        cost_estimate=pl.CostEstimate(
            flops=2 * tokens * slot_count * width, bytes_accessed=9 * 2**20, transcendentals=tokens * width // 2
        ),
        name="read_and_scores",
    )(core, *args)


def place_of(core, shifted):
    spot = [(one - core) % RING for one in shifted]
    return (spot[0] * RING + spot[1]) * RING + spot[2]


def shifted_of(core, index):
    return [(one + core) % RING for one in (index // RING**2, index // RING % RING, index % RING)]


def swap(x, axis, crossing=0):
    pairs = []
    for core in range(2):
        for index in range(RING**3):
            shifted = shifted_of(core, index)
            shifted[axis] = ((shifted[axis] + crossing) ^ 1) - crossing
            pairs.append((core * RING**3 + index, core * RING**3 + place_of(core, shifted)))
    return lax.ppermute(x, ("batch", "table"), pairs)


def swap_cores(x):
    return lax.ppermute(x, "batch", [(0, 1), (1, 0)])


def cube_exchange(x):
    groups = []
    for core in range(2):
        found = {}
        for index in range(RING**3):
            shifted = shifted_of(core, index)
            group = tuple((one + 1) % RING // 2 for one in shifted)
            order = sum(bit * (one // 2) for bit, one in zip(BITS, shifted))
            found.setdefault(group, {})[order] = core * RING**3 + index
        groups += [[members[n] for n in range(CUBE)] for _, members in sorted(found.items())]
    return lax.all_to_all(
        x, ("batch", "table"), split_axis=0, concat_axis=0, axis_index_groups=groups, tiled=True
    )


def after(first, then):
    count = len(first)
    return lax.optimization_barrier((*first, *then))[count:]


def local(
    gate_pre, pick_logits, requests, slot_of_pick, values, first_moment, second_moment, out_grad
):
    capacity, table_size = requests.shape
    slot_count = capacity * table_size
    row_count, width = values.shape
    half_width = width // 2
    core = lax.axis_index("batch")
    shifted = shifted_of(core, lax.axis_index("table"))
    inside = sum(bit * (one % 2) for bit, one in zip(BITS, shifted))
    spot = inside.astype(jnp.int32).reshape(1)
    which = core.astype(jnp.int32).reshape(1)

    mine = lax.dynamic_slice(values, (0, core * half_width), (row_count, half_width))
    parts = [mine[:, chunk * CHUNK : (chunk + 1) * CHUNK] for chunk in range(len(ORDERS))]
    swapped = [swap(part, order[0]) for part, order in zip(parts, ORDERS)]

    lists = jnp.stack([requests, swap_cores(requests)]).reshape(2, capacity, RING, RING, RING)
    for axis in range(2, 5):
        turned = jnp.concatenate(
            [lax.slice_in_dim(lists, RING - 1, RING, axis=axis), lax.slice_in_dim(lists, 0, RING - 1, axis=axis)],
            axis=axis,
        )
        lists = jnp.where(core == 0, lists, turned)
    lists = lists.reshape(2, capacity, 2, 2, 2, 2, 2, 2).transpose(2, 4, 6, 0, 3, 5, 7, 1)
    lists = lists.reshape(2 * CUBE, ROW_BLOCK).astype(jnp.float32)

    lists = lists[None]
    (which_late,) = after([lists], [which])
    crossed = swap(lists, 0, 1)
    gated, gated_theirs = gated_call(which_late, gate_pre, out_grad)
    gated_other = swap_cores(gated_theirs)
    swapped = after([gated], swapped)
    (crossed,) = after([gated], [crossed])
    lists = jnp.concatenate([lists, crossed], axis=0)
    crossed = swap(lists, 1, 1)
    parts = [jnp.concatenate(pair, axis=0) for pair in zip(parts, swapped)]
    swapped = [swap(part, order[1]) for part, order in zip(parts, ORDERS)]
    slot = (slot_of_pick % table_size) * capacity + slot_of_pick // table_size
    (slot,) = after(parts, [slot])
    packed, weight = pack_call(pick_logits, slot, slot_count)
    packed_other = swap_cores(packed)
    (crossed,) = after([packed], [crossed])
    lists = jnp.concatenate([lists, crossed], axis=0)
    crossed = swap(lists, 2, 1)
    slot_grad = slot_grad_call(which, packed, packed_other, gated, gated_other)
    swapped = after([slot_grad], swapped)
    (crossed,) = after([slot_grad], [crossed])
    (slot_grad,) = after([crossed, *swapped], [slot_grad])
    arrived = cube_exchange(slot_grad)
    parts = [jnp.concatenate(pair, axis=0) for pair in zip(parts, swapped)]
    swapped = [swap(part, order[2]) for part, order in zip(parts, ORDERS)]
    gathered = [half for pair in zip(parts, swapped) for half in pair]

    lists = jnp.concatenate([lists, crossed], axis=0)
    own_cube = sum(bit * (one // 2) for bit, one in zip(BITS, shifted))
    lists = lists.reshape(CUBE, CUBE, 2, ROW_BLOCK)
    lists = lax.dynamic_slice(lists, (0, own_cube, 0, 0), (CUBE, 1, 2, ROW_BLOCK))
    lists = lists.reshape(2, 2, 2, 2, ROW_BLOCK).transpose(2, 1, 0, 3, 4)
    for axis in range(3):
        lists = jnp.where(shifted[axis] // 2 == 0, lists, jnp.flip(lists, axis))
    ids = spread_call(lists.reshape(2 * CUBE, ROW_BLOCK))
    found_other = select_call(1, spot, ids, gathered, half_width)
    (arrived,) = after([found_other], [arrived])
    (found_other,) = after([arrived], [found_other])
    fetched_theirs = cube_exchange(found_other)

    halves = [partial_call(chunk, spot, ids, arrived, row_count) for chunk in range(len(ORDERS))]
    (ids,) = after([keep for keep, _ in halves], [ids])
    found = select_call(0, spot, ids, gathered, half_width)
    received = [swap(send, order[2]) for (_, send), order in zip(halves, ORDERS)]
    received = after([found], received)
    half = CUBE // 4 * row_count
    totals = [keep + other.astype(jnp.float32) for (keep, _), other in zip(halves, received)]
    halves = [(total[:half], total[half:].astype(jnp.bfloat16)) for total in totals]
    received = [swap(send, order[1]) for (_, send), order in zip(halves, ORDERS)]
    (fetched_theirs,) = after(received, [fetched_theirs])
    (found,) = after([fetched_theirs, *received], [found])
    fetched = cube_exchange(found)
    fetched_other = swap_cores(fetched_theirs)

    half //= 2
    totals = [keep + other.astype(jnp.float32) for (keep, _), other in zip(halves, received)]
    halves = [(total[:half], total[half:].astype(jnp.bfloat16)) for total in totals]
    received = [swap(send, order[0]) for (_, send), order in zip(halves, ORDERS)]
    layer_out, gate_grad, score = read_call(which, packed, fetched_other, gate_pre, out_grad)
    received = after([score], received)
    totals = [keep + other.astype(jnp.float32) for (keep, _), other in zip(halves, received)]
    own = jnp.concatenate(totals, axis=1)
    value_next, first_next, second_next = adam_call(
        which, own, swap_cores(own), values, first_moment, second_moment
    )
    (fetched,) = after([value_next], [fetched])
    layer_out, gate_grad, logit_grad = read_call(
        which, packed, fetched, gate_pre, out_grad, (weight, slot, layer_out, gate_grad, score)
    )
    return (layer_out, gate_grad, logit_grad.T, value_next, first_next, second_next)


def solution(mesh):
    tokens = P(("batch", "table"), None)
    rows = P("table", None)
    return jax.shard_map(
        local,
        mesh=mesh,
        in_specs=(tokens, tokens, tokens, tokens, rows, rows, rows, tokens),
        out_specs=(tokens, tokens, tokens, rows, rows, rows),
        check_vma=False,
    )
```

```python
import functools

import jax
import jax.numpy as jnp
from jax import lax
from jax.experimental import pallas as pl
from jax.experimental.pallas import tpu as pltpu
from jax.sharding import PartitionSpec as P

learn_rate = 0.001
LANES = 128
COLS = 512
RING = 4
CAPACITY = 16
CUBE = 8
BITS = (4, 2, 1)
ORDERS = ((0, 1, 2), (1, 2, 0), (2, 0, 1))
VMEM_BYTES = 60 * 1024 * 1024


CHUNK = 768
ROW_BLOCK = LANES


def chunk_width(chunk, total):
    return min(CHUNK, total - chunk * CHUNK)


def slot_place(owner, shift):
    spot = (owner // RING**2, owner // RING % RING, owner % RING)
    places = []
    for core in range(2):
        shifted = [(one + core) % RING for one in spot]
        cube = sum(bit * (one // 2) for bit, one in zip(BITS, shifted))
        chip = sum(bit * (one % 2) for bit, one in zip(BITS, shifted))
        places.append((cube, chip))
    (cube_0, chip_0), (cube_1, chip_1) = places
    cube = cube_0 + shift * (cube_1 - cube_0)
    chip = chip_0 + shift * (chip_1 - chip_0)
    return cube, chip


def pack_kernel(logit_ref, slot_ref, packed_ref, weight_ref):
    tokens, picks = logit_ref.shape
    slot_count = packed_ref.shape[1]
    logits = logit_ref[...]
    raised = jnp.exp(logits - jnp.max(logits, axis=-1, keepdims=True))
    weight_ref[...] = raised / jnp.sum(raised, axis=-1, keepdims=True)
    rows = 16

    @pl.loop(0, tokens // rows)
    def _(step):
        here = pl.ds(pl.multiple_of(step * rows, rows), rows)
        weight = weight_ref[here, :]
        slot = slot_ref[here, :]
        lane = lax.broadcasted_iota(jnp.int32, (rows, slot_count), 1)
        total = jnp.zeros((rows, slot_count), jnp.float32)
        for k in range(picks):
            total = jnp.where(lane == slot[:, k : k + 1], weight[:, k : k + 1], total)
        packed_ref[here, :] = total.astype(jnp.bfloat16)


def pack_call(logits, slot, slot_count):
    tokens, picks = logits.shape
    return pl.pallas_call(
        pack_kernel,
        out_shape=[
            jax.ShapeDtypeStruct((tokens, slot_count), jnp.bfloat16),
            jax.ShapeDtypeStruct((tokens, picks), jnp.float32),
        ],
        compiler_params=pltpu.CompilerParams(vmem_limit_bytes=VMEM_BYTES),
        cost_estimate=pl.CostEstimate(
            flops=2**25, bytes_accessed=2**20, transcendentals=tokens * picks
        ),
        name="pack_weights",
    )(logits, slot)


def gated_kernel(core_ref, gate_a, grad_a, gate_b, grad_b, mine_ref, theirs_ref):
    for gate_ref, grad_ref, out_ref in ((gate_a, grad_a, mine_ref), (gate_b, grad_b, theirs_ref)):
        gate = gate_ref[...].astype(jnp.float32)
        silu = gate * jax.nn.sigmoid(gate)
        out_ref[...] = (grad_ref[...].astype(jnp.float32) * silu).astype(jnp.bfloat16)


def gated_call(core, gate, grad):
    tokens, width = gate.shape
    steps = width // 2 // COLS
    mine = pl.BlockSpec((tokens, COLS), lambda i, core: (0, core[0] * steps + i))
    theirs = pl.BlockSpec((tokens, COLS), lambda i, core: (0, (1 - core[0]) * steps + i))
    half = pl.BlockSpec((tokens, COLS), lambda i, core: (0, i))
    return pl.pallas_call(
        gated_kernel,
        grid_spec=pltpu.PrefetchScalarGridSpec(
            num_scalar_prefetch=1,
            grid=(steps,),
            in_specs=[mine, mine, theirs, theirs],
            out_specs=[half, half],
        ),
        out_shape=[jax.ShapeDtypeStruct((tokens, width // 2), jnp.bfloat16)] * 2,
        compiler_params=pltpu.CompilerParams(vmem_limit_bytes=VMEM_BYTES),
        cost_estimate=pl.CostEstimate(
            flops=4 * tokens * width, bytes_accessed=6 * tokens * width, transcendentals=tokens * width
        ),
        name="gated_halves",
    )(core, gate, grad, gate, grad)


def slot_grad_kernel(
    core_ref, packed_ref, packed_other_ref, gated_ref, gated_other_ref, slot_grad_ref, turned_ref
):
    slot_count = packed_ref.shape[1]
    groups = ((packed_ref, gated_ref), (packed_other_ref, gated_other_ref))

    @pl.when(pl.program_id(0) == 0)
    def _():
        for group, (weights, _) in enumerate(groups):
            turned_ref[group] = weights[...].T

    for group, (_, gated) in enumerate(groups):
        found = jnp.dot(
            turned_ref[group], gated[...], preferred_element_type=jnp.float32
        ).astype(jnp.bfloat16)
        for owner in range(slot_count // CAPACITY):
            cube, chip = slot_place(owner, core_ref[0])
            start = (cube * 2 + group) * ROW_BLOCK + chip * CAPACITY
            slot_grad_ref[pl.ds(pl.multiple_of(start, CAPACITY), CAPACITY), :] = found[
                owner * CAPACITY : (owner + 1) * CAPACITY, :
            ]


def slot_grad_call(core, packed, packed_other, gated, gated_other):
    tokens, half = gated.shape
    slot_count = packed.shape[1]
    whole = lambda i: (0, 0)
    by_cols = lambda i: (0, i)
    weights = pl.BlockSpec((tokens, slot_count), whole)
    columns = pl.BlockSpec((tokens, COLS), by_cols)
    return pl.pallas_call(
        slot_grad_kernel,
        grid=(half // COLS,),
        in_specs=[pl.BlockSpec(memory_space=pltpu.SMEM), weights, weights, columns, columns],
        out_specs=pl.BlockSpec((2 * slot_count, COLS), by_cols),
        out_shape=jax.ShapeDtypeStruct((2 * slot_count, half), jnp.bfloat16),
        scratch_shapes=[pltpu.VMEM((2, slot_count, tokens), jnp.bfloat16)],
        compiler_params=pltpu.CompilerParams(vmem_limit_bytes=VMEM_BYTES),
        cost_estimate=pl.CostEstimate(
            flops=4 * tokens * slot_count * half, bytes_accessed=14 * 2**20, transcendentals=0
        ),
        name="slot_gradients",
    )(core, packed, packed_other, gated, gated_other)


def spread_kernel(list_ref, spread_ref):
    ones = jnp.ones((LANES, LANES), jnp.bfloat16)
    row = lax.broadcasted_iota(jnp.int32, (LANES, LANES), 0)
    lane = lax.broadcasted_iota(jnp.int32, (LANES, LANES), 1)
    for block in range(list_ref.shape[0]):
        diagonal = jnp.where(row == lane, list_ref[block : block + 1, :], 0.0)
        spread_ref[block * LANES : (block + 1) * LANES, :] = jnp.dot(
            diagonal.astype(jnp.bfloat16), ones, preferred_element_type=jnp.float32
        ).astype(jnp.bfloat16)


def spread_call(lists):
    return pl.pallas_call(
        spread_kernel,
        out_shape=jax.ShapeDtypeStruct((lists.size, LANES), jnp.bfloat16),
        name="spread_lists",
    )(lists)


def relative(order, position):
    return sum(BITS[axis] for bit, axis in enumerate(order) if position >> bit & 1)


def asked_at(owner, peer, group):
    start = (peer * 2 + group) * ROW_BLOCK + owner * CAPACITY
    return pl.ds(pl.multiple_of(start, CAPACITY), CAPACITY)


def asked_rows(ref, owner, groups):
    return jnp.concatenate(
        [ref[asked_at(owner, peer, group), :] for peer in range(CUBE) for group in groups], axis=0
    )


def chosen_rows(id_ref, owner, groups):
    ids = asked_rows(id_ref, owner, groups)
    lane = lax.broadcasted_iota(jnp.int32, ids.shape, 1)
    return (ids.astype(jnp.float32) == lane.astype(jnp.float32)).astype(jnp.bfloat16)


def select_kernel(group, spot_ref, id_ref, *refs):
    out_ref = refs[-1]
    for chunk, order in enumerate(ORDERS):
        near, far = refs[2 * chunk], refs[2 * chunk + 1]
        rows = near.shape[0] * 2 // CUBE

        @pl.when(pl.program_id(0) == chunk)
        def _(order=order, near=near, far=far, rows=rows):
            for position in range(CUBE):
                source = near if position < CUBE // 2 else far
                start = position % (CUBE // 2) * rows
                owner = spot_ref[0] ^ relative(order, position)
                found = jnp.dot(
                    chosen_rows(id_ref, owner, (group,)),
                    source[start : start + rows, :],
                    preferred_element_type=jnp.float32,
                ).astype(jnp.bfloat16)
                for peer in range(CUBE):
                    at = pl.ds(
                        pl.multiple_of(peer * ROW_BLOCK + owner * CAPACITY, CAPACITY), CAPACITY
                    )
                    out_ref[at, : found.shape[1]] = found[peer * CAPACITY : (peer + 1) * CAPACITY, :]


def select_call(group, spot, ids, parts, half_width):
    rows, wide = ids.shape[0], half_width + LANES
    whole = lambda i: (0, 0)
    return pl.pallas_call(
        functools.partial(select_kernel, group),
        grid=(len(ORDERS),),
        in_specs=[
            pl.BlockSpec(memory_space=pltpu.SMEM),
            pl.BlockSpec(ids.shape, whole),
        ]
        + [pl.BlockSpec(part.shape, whole) for part in parts],
        out_specs=pl.BlockSpec((rows // 2, CHUNK), lambda i: (0, i)),
        out_shape=jax.ShapeDtypeStruct((rows // 2, wide - LANES), jnp.bfloat16),
        compiler_params=pltpu.CompilerParams(vmem_limit_bytes=VMEM_BYTES),
        cost_estimate=pl.CostEstimate(
            flops=rows * LANES * wide, bytes_accessed=3 * rows * wide, transcendentals=0
        ),
        name="select_rows",
    )(spot, ids, *parts)


def partial_kernel(chunk, spot_ref, id_ref, arrived_ref, keep_ref, send_ref):
    rows = keep_ref.shape[0] * 2 // CUBE
    cols = keep_ref.shape[1]
    for position in range(CUBE):
        owner = spot_ref[0] ^ relative(ORDERS[chunk], position)
        chosen = chosen_rows(id_ref, owner, (0, 1))
        by_rows = (((0,), (0,)), ((), ()))
        total = lax.dot_general(
            chosen, asked_rows(arrived_ref, owner, (0, 1))[:, :cols], by_rows,
            preferred_element_type=jnp.float32,
        )
        target = keep_ref if position < CUBE // 2 else send_ref
        start = position % (CUBE // 2) * rows
        target[start : start + rows, :] = total.astype(target.dtype)
        if chunk == len(ORDERS) - 1:
            hits = lax.dot_general(
                chosen, jnp.ones(chosen.shape, jnp.bfloat16), by_rows, preferred_element_type=jnp.float32
            )
            target[start : start + rows, cols - LANES :] = hits.astype(target.dtype)


def partial_call(chunk, spot, ids, arrived, row_count):
    rows, wide = arrived.shape[0], arrived.shape[1] + LANES
    cols = chunk_width(chunk, wide)
    half = CUBE // 2 * row_count
    whole = lambda i: (0, 0)
    return pl.pallas_call(
        functools.partial(partial_kernel, chunk),
        grid=(1,),
        in_specs=[
            pl.BlockSpec(memory_space=pltpu.SMEM),
            pl.BlockSpec(ids.shape, whole),
            pl.BlockSpec((rows, CHUNK), lambda i: (0, chunk)),
        ],
        out_specs=[pl.BlockSpec((half, cols), whole)] * 2,
        out_shape=[
            jax.ShapeDtypeStruct((half, cols), jnp.float32),
            jax.ShapeDtypeStruct((half, cols), jnp.bfloat16),
        ],
        compiler_params=pltpu.CompilerParams(vmem_limit_bytes=VMEM_BYTES),
        cost_estimate=pl.CostEstimate(
            flops=2 * rows * LANES * cols, bytes_accessed=8 * rows * cols, transcendentals=0
        ),
        name="partial_sums",
    )(spot, ids, arrived)


def adam_kernel(
    core_ref, hits_ref, own_ref, other_ref, value_ref, first_ref, second_ref,
    value_out, first_out, second_out,
):
    touched = hits_ref[...][:, :1] > 0.0
    own = pl.program_id(0) < pl.num_programs(0) // 2
    row_grad = jnp.where(own, own_ref[...], other_ref[...])
    first = first_ref[...]
    second = second_ref[...]
    value = value_ref[...].astype(jnp.float32)
    first_new = 0.9 * first + 0.1 * row_grad
    second_new = 0.95 * second + 0.05 * row_grad * row_grad
    value_new = value - learn_rate * first_new / (jnp.sqrt(second_new) + 1e-08)
    value_out[...] = jnp.where(touched, value_new, value).astype(jnp.bfloat16)
    first_out[...] = jnp.where(touched, first_new, first)
    second_out[...] = jnp.where(touched, second_new, second)


def adam_call(core, own, other, values, first, second):
    rows, width = values.shape
    steps = width // 2 // COLS
    columns = pl.BlockSpec(
        (rows, COLS),
        lambda i, core: (0, lax.rem(core[0] + i // steps, 2) * steps + lax.rem(i, steps)),
    )
    return pl.pallas_call(
        adam_kernel,
        grid_spec=pltpu.PrefetchScalarGridSpec(
            num_scalar_prefetch=1,
            grid=(2 * steps,),
            in_specs=[
                pl.BlockSpec((rows, LANES), lambda i, core: (0, width // 2 // LANES)),
                pl.BlockSpec((rows, COLS), lambda i, core: (0, jnp.minimum(i, steps - 1))),
                pl.BlockSpec((rows, COLS), lambda i, core: (0, jnp.maximum(i - steps, 0))),
                columns, columns, columns,
            ],
            out_specs=[columns] * 3,
        ),
        out_shape=[
            jax.ShapeDtypeStruct(values.shape, values.dtype),
            jax.ShapeDtypeStruct(first.shape, first.dtype),
            jax.ShapeDtypeStruct(second.shape, second.dtype),
        ],
        compiler_params=pltpu.CompilerParams(vmem_limit_bytes=VMEM_BYTES),
        cost_estimate=pl.CostEstimate(
            flops=10 * rows * width, bytes_accessed=28 * rows * width, transcendentals=rows * width
        ),
        name="adam_rows",
    )(core, own, own, other, values, first, second)


def read_kernel(own, core_ref, packed_ref, fetched_ref, gate_ref, grad_ref, *refs):
    if own:
        weight_ref, slot_ref, before_ref, _, _, out_ref, gate_grad_ref, logit_grad_ref = refs[:8]
    else:
        out_ref, gate_grad_ref, score_out_ref = refs[:3]
    ordered_ref, score_ref = refs[-2:]
    step = pl.program_id(0)
    shift = core_ref[0] if own else 1 - core_ref[0]
    for owner in range(ordered_ref.shape[0] // CAPACITY):
        cube, chip = slot_place(owner, shift)
        at = pl.ds(pl.multiple_of(cube * ROW_BLOCK + chip * CAPACITY, CAPACITY), CAPACITY)
        ordered_ref[owner * CAPACITY : (owner + 1) * CAPACITY, :] = fetched_ref[at, :]
    fetched = ordered_ref[...]
    memory = jnp.dot(packed_ref[...], fetched, preferred_element_type=jnp.float32)
    gate = gate_ref[...].astype(jnp.float32)
    sig = jax.nn.sigmoid(gate)
    silu = gate * sig
    grad = grad_ref[...].astype(jnp.float32)
    out_ref[...] = (silu * memory).astype(jnp.bfloat16)
    gated = (grad * silu).astype(jnp.bfloat16)
    gate_grad_ref[...] = (grad * memory * sig * (1.0 + gate * (1.0 - sig))).astype(jnp.bfloat16)
    score = lax.dot_general(
        gated, fetched, (((1,), (1,)), ((), ())), preferred_element_type=jnp.float32
    )

    @pl.when(step == 0)
    def _():
        score_ref[...] = score + before_ref[...] if own else score

    @pl.when(step > 0)
    def _():
        score_ref[...] += score

    @pl.when(step == pl.num_programs(0) - 1)
    def _():
        if not own:
            score_out_ref[...] = score_ref[...]
            return
        picks = weight_ref.shape[1]
        slot = slot_ref[...]
        low = lax.rem(slot, LANES)
        high = slot // LANES
        wide = jnp.zeros(slot.shape, jnp.float32)
        for part in range(score_ref.shape[1] // LANES):
            here = score_ref[:, part * LANES : (part + 1) * LANES]
            wide = jnp.where(high == part, jnp.take_along_axis(here, low, axis=1), wide)
        pick_score = wide[:, :picks]
        weight = weight_ref[...]
        mean_score = jnp.sum(weight * pick_score, axis=-1, keepdims=True)
        wide = jnp.pad(weight * (pick_score - mean_score), ((0, 0), (0, LANES - picks)))
        logit_grad_ref[...] = wide.T[:picks, :]


def read_call(core, packed, fetched, gate, grad, last=None):
    tokens, width = gate.shape
    slot_count = packed.shape[1]
    steps = width // 2 // COLS
    own = last is not None
    whole = lambda i, core: (0, 0)

    def by_cols(i, core):
        half = core[0] if own else 1 - core[0]
        return (0, half * steps + i)

    columns = pl.BlockSpec((tokens, COLS), by_cols)
    in_specs = [
        pl.BlockSpec((tokens, slot_count), whole),
        pl.BlockSpec((slot_count, COLS), lambda i, core: (0, i)),
        columns,
        columns,
    ]
    out_specs = [columns, columns]
    out_shape = [jax.ShapeDtypeStruct((tokens, width), jnp.bfloat16)] * 2
    args = [packed, fetched, gate, grad]
    aliases = {}
    if own:
        weight, slot, layer_out, gate_grad, score = last
        picks = weight.shape[1]
        slot = jnp.pad(slot, ((0, 0), (0, LANES - picks)))
        args += [weight, slot, score, layer_out, gate_grad]
        in_specs += [pl.BlockSpec(one.shape, whole) for one in (weight, slot, score)]
        in_specs += [pl.BlockSpec(memory_space=pl.ANY)] * 2
        out_specs.append(pl.BlockSpec((picks, tokens), whole))
        out_shape.append(jax.ShapeDtypeStruct((picks, tokens), jnp.float32))
        aliases = {8: 0, 9: 1}
    else:
        out_specs.append(pl.BlockSpec((tokens, slot_count), whole))
        out_shape.append(jax.ShapeDtypeStruct((tokens, slot_count), jnp.float32))
    return pl.pallas_call(
        functools.partial(read_kernel, own),
        grid_spec=pltpu.PrefetchScalarGridSpec(
            num_scalar_prefetch=1,
            grid=(steps,),
            in_specs=in_specs,
            out_specs=out_specs,
            scratch_shapes=[
                pltpu.VMEM((slot_count, COLS), jnp.bfloat16),
                pltpu.VMEM((tokens, slot_count), jnp.float32),
            ],
        ),
        out_shape=out_shape,
        input_output_aliases=aliases,
        compiler_params=pltpu.CompilerParams(vmem_limit_bytes=VMEM_BYTES),
        cost_estimate=pl.CostEstimate(
            flops=2 * tokens * slot_count * width, bytes_accessed=9 * 2**20, transcendentals=tokens * width // 2
        ),
        name="read_and_scores",
    )(core, *args)


def place_of(core, shifted):
    spot = [(one - core) % RING for one in shifted]
    return (spot[0] * RING + spot[1]) * RING + spot[2]


def shifted_of(core, index):
    return [(one + core) % RING for one in (index // RING**2, index // RING % RING, index % RING)]


def swap(x, axis, crossing=0):
    pairs = []
    for core in range(2):
        for index in range(RING**3):
            shifted = shifted_of(core, index)
            shifted[axis] = ((shifted[axis] + crossing) ^ 1) - crossing
            pairs.append((core * RING**3 + index, core * RING**3 + place_of(core, shifted)))
    return lax.ppermute(x, ("batch", "table"), pairs)


def swap_cores(x):
    return lax.ppermute(x, "batch", [(0, 1), (1, 0)])


def cube_exchange(x):
    groups = []
    for core in range(2):
        found = {}
        for index in range(RING**3):
            shifted = shifted_of(core, index)
            group = tuple((one + 1) % RING // 2 for one in shifted)
            order = sum(bit * (one // 2) for bit, one in zip(BITS, shifted))
            found.setdefault(group, {})[order] = core * RING**3 + index
        groups += [[members[n] for n in range(CUBE)] for _, members in sorted(found.items())]
    return lax.all_to_all(
        x, ("batch", "table"), split_axis=0, concat_axis=0, axis_index_groups=groups, tiled=True
    )


def after(first, then):
    count = len(first)
    return lax.optimization_barrier((*first, *then))[count:]


def local(
    gate_pre, pick_logits, requests, slot_of_pick, values, first_moment, second_moment, out_grad
):
    capacity, table_size = requests.shape
    slot_count = capacity * table_size
    row_count, width = values.shape
    half_width = width // 2
    core = lax.axis_index("batch")
    shifted = shifted_of(core, lax.axis_index("table"))
    inside = sum(bit * (one % 2) for bit, one in zip(BITS, shifted))
    spot = inside.astype(jnp.int32).reshape(1)
    which = core.astype(jnp.int32).reshape(1)

    mine = lax.dynamic_slice(values, (0, core * half_width), (row_count, half_width))
    parts = [mine[:, chunk * CHUNK : (chunk + 1) * CHUNK] for chunk in range(len(ORDERS))]
    swapped = [swap(part, order[0]) for part, order in zip(parts, ORDERS)]

    lists = jnp.stack([requests, swap_cores(requests)]).reshape(2, capacity, RING, RING, RING)
    for axis in range(2, 5):
        turned = jnp.concatenate(
            [lax.slice_in_dim(lists, RING - 1, RING, axis=axis), lax.slice_in_dim(lists, 0, RING - 1, axis=axis)],
            axis=axis,
        )
        lists = jnp.where(core == 0, lists, turned)
    lists = lists.reshape(2, capacity, 2, 2, 2, 2, 2, 2).transpose(2, 4, 6, 0, 3, 5, 7, 1)
    lists = lists.reshape(2 * CUBE, ROW_BLOCK).astype(jnp.float32)

    lists = lists[None]
    (which_late,) = after([lists], [which])
    crossed = swap(lists, 0, 1)
    gated, gated_theirs = gated_call(which_late, gate_pre, out_grad)
    gated_other = swap_cores(gated_theirs)
    swapped = after([gated], swapped)
    (crossed,) = after([gated], [crossed])
    lists = jnp.concatenate([lists, crossed], axis=0)
    crossed = swap(lists, 1, 1)
    parts = [jnp.concatenate(pair, axis=0) for pair in zip(parts, swapped)]
    swapped = [swap(part, order[1]) for part, order in zip(parts, ORDERS)]
    slot = (slot_of_pick % table_size) * capacity + slot_of_pick // table_size
    (slot,) = after([*parts, lists], [slot])
    packed, weight = pack_call(pick_logits, slot, slot_count)
    packed_other = swap_cores(packed)
    (crossed,) = after([packed], [crossed])
    lists = jnp.concatenate([lists, crossed], axis=0)
    crossed = swap(lists, 2, 1)
    slot_grad = slot_grad_call(which, packed, packed_other, gated, gated_other)
    swapped = after([slot_grad], swapped)
    (crossed,) = after([slot_grad], [crossed])
    (slot_grad,) = after([crossed, *swapped], [slot_grad])
    arrived = cube_exchange(slot_grad)
    parts = [jnp.concatenate(pair, axis=0) for pair in zip(parts, swapped)]
    swapped = [swap(part, order[2]) for part, order in zip(parts, ORDERS)]
    gathered = [half for pair in zip(parts, swapped) for half in pair]

    lists = jnp.concatenate([lists, crossed], axis=0)
    own_cube = sum(bit * (one // 2) for bit, one in zip(BITS, shifted))
    lists = lists.reshape(CUBE, CUBE, 2, ROW_BLOCK)
    lists = lax.dynamic_slice(lists, (0, own_cube, 0, 0), (CUBE, 1, 2, ROW_BLOCK))
    lists = lists.reshape(2, 2, 2, 2, ROW_BLOCK).transpose(2, 1, 0, 3, 4)
    for axis in range(3):
        lists = jnp.where(shifted[axis] // 2 == 0, lists, jnp.flip(lists, axis))
    ids = spread_call(lists.reshape(2 * CUBE, ROW_BLOCK))
    found_other = select_call(1, spot, ids, gathered, half_width)
    (arrived,) = after([found_other], [arrived])
    (found_other,) = after([arrived], [found_other])
    fetched_theirs = cube_exchange(found_other)

    halves = [partial_call(chunk, spot, ids, arrived, row_count) for chunk in range(len(ORDERS))]
    (ids,) = after([keep for keep, _ in halves], [ids])
    found = select_call(0, spot, ids, gathered, half_width)
    received = [swap(send, order[2]) for (_, send), order in zip(halves, ORDERS)]
    received = after([found], received)
    half = CUBE // 4 * row_count
    totals = [keep + other.astype(jnp.float32) for (keep, _), other in zip(halves, received)]
    halves = [(total[:half], total[half:].astype(jnp.bfloat16)) for total in totals]
    received = [swap(send, order[1]) for (_, send), order in zip(halves, ORDERS)]
    (fetched_theirs,) = after([send for _, send in halves], [fetched_theirs])
    (found,) = after([fetched_theirs, *received], [found])
    fetched = cube_exchange(found)
    fetched_other = swap_cores(fetched_theirs)

    half //= 2
    totals = [keep + other.astype(jnp.float32) for (keep, _), other in zip(halves, received)]
    halves = [(total[:half], total[half:].astype(jnp.bfloat16)) for total in totals]
    received = [swap(send, order[0]) for (_, send), order in zip(halves, ORDERS)]
    layer_out, gate_grad, score = read_call(which, packed, fetched_other, gate_pre, out_grad)
    received = after([score], received)
    totals = [keep + other.astype(jnp.float32) for (keep, _), other in zip(halves, received)]
    own = jnp.concatenate(totals, axis=1)
    value_next, first_next, second_next = adam_call(
        which, own, swap_cores(own), values, first_moment, second_moment
    )
    (fetched,) = after([value_next], [fetched])
    layer_out, gate_grad, logit_grad = read_call(
        which, packed, fetched, gate_pre, out_grad, (weight, slot, layer_out, gate_grad, score)
    )
    return (layer_out, gate_grad, logit_grad.T, value_next, first_next, second_next)


def solution(mesh):
    tokens = P(("batch", "table"), None)
    rows = P("table", None)
    return jax.shard_map(
        local,
        mesh=mesh,
        in_specs=(tokens, tokens, tokens, tokens, rows, rows, rows, tokens),
        out_specs=(tokens, tokens, tokens, rows, rows, rows),
        check_vma=False,
    )
```
